32 devices in a mesh: grp: 4 (over x, core), dev: 8 (over z, y).
Axes of the slice: x: 2, y: 2, z: 4, core: 2. Of those that a mesh axis runs over, the one named last changes fastest.
Arguments:
- ref_pos: float32 [3, 262144], P(None, ('grp', 'dev')), may hold values from -4 to 4
- displacement: float32 [3, 262144], P(None, ('grp', 'dev')), may hold values from -0.6 to 0.6
- velocity: float32 [3, 262144], P(None, ('grp', 'dev')), may hold values from -6 to 6
- node_mass: float32 [262144], P(('grp', 'dev')), may hold values from 0.5 to 2
- elem_nodes: int32 [4, 262144], P(None, ('grp', 'dev')), may hold values from 0 to 8191
- elem_part: int32 [262144], P(('grp', 'dev')), may hold values from 0 to 127, as said below
- elem_scale: float32 [262144], P(('grp', 'dev')), may hold values from 0.5 to 2
- part_stiff: float32 [128], P(('grp', 'dev')), may hold values from 1 to 100
- shared: int32 [2, 65536], P(None, ('grp', 'dev')), may hold values from 0 to 8191, as said below
- seg_node: int32 [2048, 128], P(('grp', 'dev')), may hold values from 0 to 8191
- seg_mask: int32 [2048, 128], P(('grp', 'dev')), may hold values 0 or 1
- send_blk: int32 [32, 32, 5], P(('grp', 'dev')), may hold values from 0 to 63
- pair_a: int32 [16384], P(('grp', 'dev')), may hold values from 0 to 63
- pair_slot: int32 [16384], P(('grp', 'dev')), may hold values from 0 to 159
- pair_mask: int32 [16384], P(('grp', 'dev')), may hold values from 0 to 1, as said below
Outputs:
- new_displace: float32 [3, 262144], P(None, ('grp', 'dev'))
- new_velocity: float32 [3, 262144], P(None, ('grp', 'dev'))
The draws below stay inside these ranges and needn't reach their ends.
Inputs may be any that keep to these rules, and one draw needn't show every extreme that they name: `elem_part`: the elements of device d belong to parts d * 4 to (d + 1) * 4 - 1. `shared`: the 4096 entries of one device are different nodes; row 1 of device k and row 0 of device k + 1 of the same group name the same physical nodes, entry by entry. `pair_mask`: in each device's 512 pair slots the live ones come first; each device has 128 or more live, and some device has all 512 live.
All inputs are finite; a program needn't handle non-finite values. No bound on the sum of `seg_mask` on one device may be relied on, other than what follows from the above.
Results may differ from the reference program's by a relative error of at most 0.000062.
Values sent between devices are 32-bit elements; how exact they have to be, the bound alone decides.
A program may use at most 128 MiB of HBM per device.

```python
import math
import jax
import jax.numpy as jnp
from jax import lax

NODE_DEV = 8192
SHARE = 2048
BLK_DEV = 64
PAIR_DEV = 512
SEG = 128
CAP = 5
PART_DEV = 4
ELEM_DEV = 8192
NODES = 262144
ELEMS = 262144
BLOCKS = 2048
PAIRS = 16384
PARTS_SIZE = 128
N_GRP = 4
N_DEV = 8
DEVICES = 32


def draw_elem_part(key, part):
    owner_device = jnp.arange(ELEMS, dtype=jnp.int32) // ELEM_DEV
    offset = jax.random.randint(key, (ELEMS,), 0, PART_DEV, dtype=jnp.int32)
    return owner_device * PART_DEV + offset


def draw_shared(key, part):
    device_count = NODES // NODE_DEV
    device_keys = jax.random.split(jax.random.fold_in(key, 11), device_count)

    def one_device(device_key):
        return jax.random.permutation(device_key, NODE_DEV)[:2 * SHARE].astype(jnp.int32)
    picked = jax.vmap(one_device)(device_keys)
    return jnp.moveaxis(picked.reshape(device_count, 2, SHARE), 1, 0).reshape(2, device_count * SHARE)


def draw_pair_mask(key, part):
    device_count = PAIRS // PAIR_DEV
    live_key, full_key = jax.random.split(jax.random.fold_in(key, 23))
    live_count = jax.random.randint(live_key, (device_count,), PAIR_DEV // 4, PAIR_DEV + 1, dtype=jnp.int32)
    full_device = jax.random.randint(full_key, (), 0, device_count, dtype=jnp.int32)
    live_count = jnp.where(jnp.arange(device_count, dtype=jnp.int32) == full_device, PAIR_DEV, live_count)
    positions = jnp.arange(PAIR_DEV, dtype=jnp.int32)
    return (positions[None, :] < live_count[:, None]).astype(jnp.int32).reshape(-1)


def touch_ends(drawn, rng, low, top_value):
    shape = drawn.shape
    spot = [jax.random.randint(jax.random.fold_in(rng, axis), (), 0, shape[axis]) for axis in range(len(shape))]
    drawn = drawn.at[tuple(spot)].set(low)
    longest = shape.index(max(shape))
    spot[longest] = (spot[longest] + 1) % shape[longest]
    return drawn.at[tuple(spot)].set(top_value)


def block_levels(own_key, extent, shards, low, high):
    def one(dim, shards_of):
        steps = jax.random.uniform(jax.random.fold_in(jax.random.fold_in(own_key, 6), dim), (shards_of,), jnp.float32, low / len(shards), high / len(shards))
        return jnp.repeat(jnp.exp(steps), extent[dim] // shards_of).reshape((-1,) + (1,) * (len(extent) - dim - 1))

    level = one(*shards[0])
    for cut in shards[1:]:
        level = level * one(*cut)
    return level


def centred(key, extent, scale, most, cuts=(), kind=jnp.bfloat16):
    result = scale * jax.random.normal(key, extent, jnp.float32)
    if cuts:
        result = result * block_levels(key, extent, cuts, -0.22, 0.18)
    return jnp.clip(result, -most, most).astype(kind)


def setup_inputs(seed: int = 0) -> dict:
    seeds = jax.random.split(jax.random.key(seed), 16)
    return {
        "ref_pos": centred(seeds[0], (3, NODES), 0.7, 4.0, ((1, 32),), jnp.float32),
        "displacement": centred(seeds[1], (3, NODES), 0.1, 0.6, ((1, 32),), jnp.float32),
        "velocity": centred(seeds[2], (3, NODES), 1.0, 6.0, ((1, 32),), jnp.float32),
        "node_mass": jnp.clip(jnp.exp(math.log(2.0) - 1.3862944 * jax.random.uniform(seeds[3], (NODES,), jnp.float32) ** block_levels(seeds[3], (NODES,), ((0, 32),), -0.2, 0.2)), 0.5, 2.0),
        "elem_nodes": touch_ends(jax.random.randint(seeds[4], (4, ELEMS), 0, NODE_DEV), jax.random.fold_in(seeds[4], 1), 0, NODE_DEV - 1).astype(jnp.int32),
        "elem_part": draw_elem_part(jax.random.fold_in(seeds[15], 71), 0),
        "elem_scale": jnp.clip(jnp.exp(math.log(2.0) - 1.3862944 * jax.random.uniform(seeds[6], (ELEMS,), jnp.float32) ** block_levels(seeds[6], (ELEMS,), ((0, 32),), -0.2, 0.2)), 0.5, 2.0),
        "part_stiff": jnp.clip(jnp.exp(math.log(100.0) - 4.6051702 * jax.random.uniform(seeds[7], (PARTS_SIZE,), jnp.float32) ** block_levels(seeds[7], (PARTS_SIZE,), ((0, 32),), -0.2, 0.2)), 1.0, 100.0),
        "shared": draw_shared(jax.random.fold_in(seeds[15], 71), 0),
        "seg_node": touch_ends(jax.random.randint(seeds[9], (BLOCKS, SEG), 0, NODE_DEV), jax.random.fold_in(seeds[9], 1), 0, NODE_DEV - 1).astype(jnp.int32),
        "seg_mask": touch_ends((jax.random.randint(seeds[10], (BLOCKS, SEG), 0, 8) < 7).astype(jnp.int32), jax.random.fold_in(seeds[10], 1), 0, 1),
        "send_blk": touch_ends(jax.random.randint(seeds[11], (DEVICES, DEVICES, CAP), 0, BLK_DEV), jax.random.fold_in(seeds[11], 1), 0, BLK_DEV - 1).astype(jnp.int32),
        "pair_a": touch_ends(jax.random.randint(seeds[12], (PAIRS,), 0, BLK_DEV), jax.random.fold_in(seeds[12], 1), 0, BLK_DEV - 1).astype(jnp.int32),
        "pair_slot": touch_ends(jax.random.randint(seeds[13], (PAIRS,), 0, DEVICES * CAP), jax.random.fold_in(seeds[13], 1), 0, (DEVICES * CAP) - 1).astype(jnp.int32),
        "pair_mask": draw_pair_mask(jax.random.fold_in(seeds[15], 71), 0),
    }


SPRINGS = ((0, 1, 1.0), (1, 2, 1.0), (2, 3, 1.0), (3, 0, 1.0), (0, 2, 0.5), (1, 3, 0.5))
COURANT = 0.5

def element_forces(displacement, elem_nodes, elem_stiff):
    corner = displacement[:, elem_nodes]
    corner_force = [jnp.zeros_like(corner[:, 0]) for corner_index in range(4)]
    for head_node, tail_node, weight in SPRINGS:
        pull_term = weight * elem_stiff * (corner[:, tail_node] - corner[:, head_node])
        corner_force[head_node] = corner_force[head_node] + pull_term
        corner_force[tail_node] = corner_force[tail_node] - pull_term
    stacked = jnp.stack(corner_force, 1)
    summed = jnp.zeros_like(displacement)
    return summed.at[:, elem_nodes.reshape(-1)].add(stacked.reshape(3, -1))

def pair_forces(near_pos, far_pos, near_mask, far_mask, live_pair):
    offset = near_pos[:, :, :, None] - far_pos[:, :, None, :]
    weights = jnp.exp(-lax.optimization_barrier(jnp.sum(offset * offset, 1)))
    weights = weights * (near_mask[:, :, None] * far_mask[:, None, :]) * live_pair[:, None, None]
    pushed = lax.optimization_barrier(jnp.sum(weights[:, None] * offset, 3))
    recoil = -lax.optimization_barrier(jnp.sum(weights[:, None] * offset, 2))
    return (pushed, recoil)

def contact_sums(own_blocks, own_mask, recv_blocks, recv_mask, pair_first, pair_second, pair_live):
    pair_count = pair_first.shape[0]
    group_width = math.gcd(pair_count, 32)
    seg_width = own_blocks.shape[2]

    def one_group(group_index):
        group_start = group_index * group_width
        first_ids = lax.dynamic_slice_in_dim(pair_first, group_start, group_width)
        second_ids = lax.dynamic_slice_in_dim(pair_second, group_start, group_width)
        live_part = lax.dynamic_slice_in_dim(pair_live, group_start, group_width)
        return pair_forces(own_blocks[first_ids], recv_blocks[second_ids], own_mask[first_ids], recv_mask[second_ids], live_part)
    pushed, recoil = lax.map(one_group, jnp.arange(pair_count // group_width, dtype=jnp.int32))
    pushed = pushed.reshape(pair_count, 3, seg_width)
    recoil = recoil.reshape(pair_count, 3, seg_width)
    own_force = jax.ops.segment_sum(pushed, pair_first, num_segments=own_blocks.shape[0])
    far_force = jax.ops.segment_sum(recoil, pair_second, num_segments=recv_blocks.shape[0])
    return (own_force, far_force)

def reference(ref_pos, displacement, velocity, node_mass, elem_nodes, elem_part, elem_scale, part_stiff, shared, seg_node, seg_mask, send_blk, pair_a, pair_slot, pair_mask):
    devices = N_GRP * N_DEV
    elem_stiff = part_stiff[elem_part] * elem_scale

    def by_device(array, per_device):
        shaped = array.reshape(array.shape[:-1] + (devices, per_device))
        return jnp.moveaxis(shaped, -2, 0)
    ref_dev = by_device(ref_pos, NODE_DEV)
    disp_dev = by_device(displacement, NODE_DEV)
    vel_dev = by_device(velocity, NODE_DEV)
    mass_dev = by_device(node_mass, NODE_DEV)
    nodes_dev = by_device(elem_nodes, ELEM_DEV)
    stiff_dev = by_device(elem_stiff, ELEM_DEV)
    shared_dev = by_device(shared, SHARE)
    seg_dev = seg_node.reshape(devices, BLK_DEV, SEG)
    mask_dev = seg_mask.astype(jnp.float32).reshape(devices, BLK_DEV, SEG)
    first_dev = pair_a.reshape(devices, PAIR_DEV)
    second_dev = pair_slot.reshape(devices, PAIR_DEV)
    live_dev = pair_mask.astype(jnp.float32).reshape(devices, PAIR_DEV)

    def local_step(pieces):
        ref_local, disp_local, mass_local, nodes_local, stiff_local, seg_local = pieces
        forces = element_forces(disp_local, nodes_local, stiff_local)
        elem_mass = lax.optimization_barrier(jnp.min(mass_local[nodes_local], 0))
        step_limit = jnp.min(COURANT * jnp.sqrt(elem_mass / stiff_local))
        position = ref_local + disp_local
        blocks = jnp.moveaxis(position[:, seg_local], 1, 0)
        return (forces, step_limit, blocks)
    forces, limits, blocks = lax.map(local_step, (ref_dev, disp_dev, mass_dev, nodes_dev, stiff_dev, seg_dev))
    time_step = jnp.min(limits)
    source_ids = jnp.arange(devices, dtype=jnp.int32)[:, None]

    def contact_step(device_index):
        chosen = send_blk[:, device_index, :]
        arrived = blocks[source_ids, chosen].reshape(devices * CAP, 3, SEG)
        arrived_mask = mask_dev[source_ids, chosen].reshape(devices * CAP, SEG)
        return contact_sums(blocks[device_index], mask_dev[device_index], arrived, arrived_mask, first_dev[device_index], second_dev[device_index], live_dev[device_index])
    own_force, far_force = lax.map(contact_step, jnp.arange(devices, dtype=jnp.int32))

    def return_step(device_index):
        slab_force = lax.dynamic_slice_in_dim(far_force, device_index * CAP, CAP, 1)
        return jax.ops.segment_sum(slab_force.reshape(devices * CAP, 3, SEG), send_blk[device_index].reshape(-1), num_segments=BLK_DEV)
    returned = lax.map(return_step, jnp.arange(devices, dtype=jnp.int32))
    seg_force = own_force + returned

    def node_step(pieces):
        force_local, seg_local, seg_local_force = pieces
        flat_force = jnp.moveaxis(seg_local_force, 1, 0).reshape(3, -1)
        return force_local.at[:, seg_local.reshape(-1)].add(flat_force)
    totals = lax.map(node_step, (forces, seg_dev, seg_force))
    shaped = totals.reshape(N_GRP, N_DEV, 3, NODE_DEV)
    share_grid = shared_dev.reshape(N_GRP, N_DEV, 2, SHARE)

    def pick_rows(force_local, index_list):
        return force_local[:, index_list]
    picker = jax.vmap(jax.vmap(pick_rows))
    right_rows = picker(shaped, share_grid[:, :, 1])
    left_rows = picker(shaped, share_grid[:, :, 0])
    zero_rows = jnp.zeros_like(right_rows[:, :1])
    from_lower = jnp.concatenate([zero_rows, right_rows[:, :-1]], 1)
    from_upper = jnp.concatenate([left_rows[:, 1:], zero_rows], 1)

    def place_rows(force_local, index_list, lower_part, upper_part):
        return force_local.at[:, index_list[0]].add(lower_part).at[:, index_list[1]].add(upper_part)
    assembled = jax.vmap(jax.vmap(place_rows))(shaped, share_grid, from_lower, from_upper)
    assembled = assembled.reshape(devices, 3, NODE_DEV)
    accelerate = assembled / mass_dev[:, None, :]
    new_velocity = vel_dev + time_step * accelerate
    new_displace = disp_dev + time_step * new_velocity
    return (jnp.moveaxis(new_displace, 0, 1).reshape(3, -1), jnp.moveaxis(new_velocity, 0, 1).reshape(3, -1))
```

```python
import functools
import math

import jax
import jax.numpy as jnp
from jax import lax
from jax.experimental import pallas as pl
from jax.experimental.pallas import tpu as pltpu
from jax.sharding import PartitionSpec as P

SPRINGS = ((0, 1, 1.0), (1, 2, 1.0), (2, 3, 1.0), (3, 0, 1.0), (0, 2, 0.5), (1, 3, 0.5))
COURANT = 0.5
LOG2E = 1.4426950408889634
FAR_AWAY = 64.0
WIDE = 256
LIMIT = 48 * 1024 * 1024
F32 = jnp.float32
BF16 = jnp.bfloat16
VMEM = pl.BlockSpec(memory_space=pltpu.VMEM)
SMEM = pl.BlockSpec(memory_space=pltpu.SMEM)
PARAMS = pltpu.CompilerParams(vmem_limit_bytes=LIMIT)


def shifted(value, axis, steps):
    count = lax.axis_size(axis)
    first, last = (max(0, -steps), min(count, count - steps))
    return lax.ppermute(value, axis, [(source, source + steps) for source in range(first, last)])


def split3(x):
    first = x.astype(BF16).astype(F32)
    rest = x - first
    second = rest.astype(BF16).astype(F32)
    third = (rest - second).astype(BF16).astype(F32)
    return first, second, third


def split_table(table):
    return jnp.concatenate(split3(table), 0).astype(BF16)


def selectors(index, depth):
    count = index.shape[1]
    low = index & (WIDE - 1)
    high = index // WIDE
    hot = jnp.where(lax.broadcasted_iota(jnp.int32, (WIDE, count), 0) == low, 1.0, 0.0)
    mask = lax.broadcasted_iota(jnp.int32, (depth, count), 0) == high
    return hot.astype(BF16), mask


def pick(table, hot, mask):
    depth = mask.shape[0]
    size = table.shape[0] // 3
    parts = jnp.dot(table, hot, preferred_element_type=F32)
    whole = parts[:size] + parts[size : 2 * size] + parts[2 * size :]
    return [
        jnp.sum(jnp.where(mask, whole[row : row + depth], 0.0), 0, keepdims=True)
        for row in range(0, size, depth)
    ]


def spread(rows, hot, mask):
    firsts, seconds = [], []
    for row in rows:
        first = row.astype(BF16).astype(F32)
        firsts.append(jnp.where(mask, first, 0.0))
        seconds.append(jnp.where(mask, row - first, 0.0))
    stacked = jnp.concatenate(firsts + seconds, 0).astype(BF16)
    sums = lax.dot_general(stacked, hot, (((1,), (1,)), ((), ())), preferred_element_type=F32)
    half = sums.shape[0] // 2
    return sums[:half] + sums[half:]


def lane_row(ref, start, count):
    tile = ref[pl.ds(pl.multiple_of(start, 8), count), :]
    return jnp.concatenate([tile[row : row + 1] for row in range(count)], 1)


def segment_kernel(cap, pos_ref, disp_ref, seg_ref, mask_ref, send_ref, own_ref, out_ref):
    depth = pos_ref.shape[0] // 3
    blocks, width = seg_ref.shape
    table = split_table(pos_ref[...] + disp_ref[...])

    def gather(step, carry):
        start = step * 8
        hot, mask = selectors(lane_row(seg_ref, start, 8), depth)
        live = lane_row(mask_ref, start, 8) > 0
        rows = [jnp.where(live, row, -FAR_AWAY) for row in pick(table, hot, mask)]
        square = rows[0] * rows[0] + rows[1] * rows[1] + rows[2] * rows[2]
        rows += [jnp.ones_like(square), -LOG2E * square]
        for block in range(8):
            lanes = slice(block * width, (block + 1) * width)
            for row in range(5):
                own_ref[start + block, row : row + 1, :] = rows[row][:, lanes]
            own_ref[start + block, 5:8, :] = jnp.zeros((3, width), F32)
        return carry

    lax.fori_loop(0, blocks // 8, gather, 0)

    def send(peer, carry):
        for slot in range(cap):
            block = own_ref[send_ref[peer * cap + slot], 0:3, :]
            out_ref[peer, 3 * slot : 3 * slot + 3, :] = jnp.where(
                block < -0.5 * FAR_AWAY, FAR_AWAY, block
            )
        out_ref[peer, 3 * cap :, :] = jnp.zeros((out_ref.shape[1] - 3 * cap, width), F32)
        return carry

    lax.fori_loop(0, out_ref.shape[0], send, 0)


def element_kernel(
    chunk, disp_ref, mass_ref, nodes_ref, part_ref, scale_ref, stiff_ref, force_ref, ratio_ref
):
    depth = mass_ref.shape[0]
    elems = nodes_ref.shape[1]
    parts = stiff_ref.shape[0]
    table = split_table(jnp.concatenate([disp_ref[...], mass_ref[...]], 0))
    force_ref[...] = jnp.zeros_like(force_ref)

    def one_chunk(step, best):
        lanes = pl.ds(pl.multiple_of(step * chunk, chunk), chunk)
        local = lax.rem(part_ref[:, lanes], parts)
        stiff = jnp.zeros(local.shape, F32)
        for part in range(parts):
            stiff = jnp.where(local == part, stiff_ref[part], stiff)
        stiff = stiff * scale_ref[:, lanes]
        index = jnp.concatenate([nodes_ref[k : k + 1, lanes] for k in range(4)], 1)
        hot, mask = selectors(index, depth)
        rows = pick(table, hot, mask)
        corner = [[row[:, k * chunk : (k + 1) * chunk] for row in rows] for k in range(4)]
        mass = jnp.minimum(
            jnp.minimum(corner[0][3], corner[1][3]), jnp.minimum(corner[2][3], corner[3][3])
        )
        total = [[jnp.zeros_like(stiff) for axis in range(3)] for k in range(4)]
        for head, tail, weight in SPRINGS:
            for axis in range(3):
                pull = weight * stiff * (corner[tail][axis] - corner[head][axis])
                total[head][axis] = total[head][axis] + pull
                total[tail][axis] = total[tail][axis] - pull
        rows = [jnp.concatenate([total[k][axis] for k in range(4)], 1) for axis in range(3)]
        force_ref[...] += spread(rows, hot, mask)
        return jnp.minimum(best, mass / stiff)

    best = lax.fori_loop(
        0, elems // chunk, one_chunk, jnp.full((1, chunk), jnp.inf, F32)
    )
    ratio_ref[...] = jnp.broadcast_to(jnp.min(best, 1, keepdims=True), ratio_ref.shape)


def pair_kernel(
    cap,
    group,
    own_ref,
    got_ref,
    ratio_ref,
    first_ref,
    second_ref,
    live_ref,
    seg_ref,
    back_ref,
    near_turn,
    near_cols,
    far_rows,
    far_cols,
    near_sum,
    far_sum,
    tile_ref,
):
    blocks, _, width = own_ref.shape
    peers = got_ref.shape[0]
    pairs = first_ref.shape[0]

    def doubled(parts):
        stacked = jnp.concatenate(parts + [jnp.zeros_like(parts[0])], 0)
        return jnp.concatenate([stacked, stacked], 1).astype(BF16)

    def prepare_near(block, carry):
        one, two, three = split3(own_ref[block])
        near_turn[block] = jnp.concatenate([one, one, two, two, one, three], 0).T.astype(BF16)
        near_cols[block] = doubled([one, two, three])
        near_sum[block] = jnp.zeros((8, width), F32)
        return carry

    lax.fori_loop(0, blocks, prepare_near, 0)

    row_id = lax.broadcasted_iota(jnp.int32, (8, width), 0)
    tile_ref[...] = jnp.zeros_like(tile_ref)

    def prepare_far(peer, carry):
        for slot in range(cap):
            tile_ref[slot, 0:3, :] = got_ref[peer, 3 * slot : 3 * slot + 3, :]
        for slot in range(cap):
            tile = tile_ref[slot]
            square = -LOG2E * jnp.sum(tile * tile, 0, keepdims=True)
            scaled = jnp.where(
                row_id == 3, square, jnp.where(row_id == 4, 1.0, (2.0 * LOG2E) * tile)
            )
            one, two, three = split3(scaled)
            place = peer * cap + slot
            far_rows[place] = jnp.concatenate([one, two, one, two, three, one], 0).astype(BF16)
            far_cols[place] = doubled(list(split3(jnp.where(row_id == 3, 1.0, tile))))
            far_sum[place] = jnp.zeros((8, width), F32)
        return carry

    lax.fori_loop(0, peers, prepare_far, 0)

    def one_group(step, carry):
        results = []
        for member in range(group):
            place = step * group + member
            near, far = first_ref[place], second_ref[place]
            live = live_ref[place].astype(F32)
            power = jnp.dot(near_turn[near], far_rows[far], preferred_element_type=F32)
            weight = jnp.exp2(power)
            first = weight.astype(BF16)
            second = (weight - first.astype(F32)).astype(BF16)
            pushed = lax.dot_general(
                far_cols[far],
                jnp.concatenate([first, second], 1),
                (((1,), (1,)), ((), ())),
                preferred_element_type=F32,
            )
            recoil = jnp.dot(
                near_cols[near],
                jnp.concatenate([first, second], 0),
                preferred_element_type=F32,
            )
            pushed = live * (pushed[0:8] + pushed[8:16] + pushed[16:24])
            recoil = live * (recoil[0:8] + recoil[8:16] + recoil[16:24])
            results.append((near, far, pushed, recoil))
        for near, far, pushed, recoil in results:
            near_sum[near] += pushed
            far_sum[far] += recoil
        return carry

    lax.fori_loop(0, pairs // group, one_group, 0)

    def finish_near(block, carry):
        sums = near_sum[block]
        seg_ref[block] = own_ref[block] * sums[3:4] - sums
        return carry

    lax.fori_loop(0, blocks, finish_near, 0)

    def finish_far(peer, carry):
        for slot in range(cap):
            rows = slice(3 * slot, 3 * slot + 3)
            sums = far_sum[peer * cap + slot]
            back_ref[peer, rows, :] = got_ref[peer, rows, :] * sums[3:4] - sums[0:3]
        back_ref[peer, 3 * cap :, :] = jnp.broadcast_to(
            ratio_ref[0:1], (back_ref.shape[1] - 3 * cap, width)
        )
        return carry

    lax.fori_loop(0, peers, finish_far, 0)


def total_kernel(
    cap,
    chunk,
    back_ref,
    send_ref,
    own_ref,
    seg_ref,
    force_ref,
    shared_ref,
    total_ref,
    lower_ref,
    upper_ref,
    step_ref,
    sums,
):
    depth = force_ref.shape[0] // 3
    blocks, width = seg_ref.shape
    sums[...] = own_ref[...]

    def give_back(peer, best):
        for slot in range(cap):
            block = send_ref[peer * cap + slot]
            sums[block, 0:3, :] += back_ref[peer, 3 * slot : 3 * slot + 3, :]
        return jnp.minimum(best, back_ref[peer, 3 * cap : 3 * cap + 1, :])

    best = lax.fori_loop(
        0, back_ref.shape[0], give_back, jnp.full((1, width), jnp.inf, F32)
    )
    step_ref[...] = jnp.broadcast_to(COURANT * jnp.sqrt(best), step_ref.shape)
    total_ref[...] = force_ref[...]

    def scatter(step, carry):
        start = step * 8
        hot, mask = selectors(lane_row(seg_ref, start, 8), depth)
        rows = [
            jnp.concatenate([sums[start + block, row : row + 1, :] for block in range(8)], 1)
            for row in range(3)
        ]
        total_ref[...] += spread(rows, hot, mask)
        return carry

    lax.fori_loop(0, blocks // 8, scatter, 0)

    table = split_table(total_ref[...])

    def gather(step, carry):
        lanes = pl.ds(pl.multiple_of(step * chunk, chunk), chunk)
        for side, out_ref in ((0, upper_ref), (1, lower_ref)):
            hot, mask = selectors(shared_ref[side : side + 1, lanes], depth)
            rows = pick(table, hot, mask)
            for row in range(3):
                out_ref[row : row + 1, lanes] = rows[row]
        return carry

    lax.fori_loop(0, shared_ref.shape[1] // chunk, gather, 0)


def update_kernel(
    chunk,
    total_ref,
    lower_ref,
    upper_ref,
    shared_ref,
    mass_ref,
    vel_ref,
    disp_ref,
    step_ref,
    new_disp_ref,
    new_vel_ref,
):
    depth = mass_ref.shape[0]
    new_vel_ref[...] = total_ref[...]

    def scatter(step, carry):
        lanes = pl.ds(pl.multiple_of(step * chunk, chunk), chunk)
        for side, in_ref in ((0, lower_ref), (1, upper_ref)):
            hot, mask = selectors(shared_ref[side : side + 1, lanes], depth)
            rows = [in_ref[row : row + 1, lanes] for row in range(3)]
            new_vel_ref[...] += spread(rows, hot, mask)
        return carry

    lax.fori_loop(0, shared_ref.shape[1] // chunk, scatter, 0)
    time_step = step_ref[0:1, 0:1]
    mass = mass_ref[...]
    for axis in range(3):
        rows = slice(axis * depth, (axis + 1) * depth)
        velocity = vel_ref[rows, :] + time_step * (new_vel_ref[rows, :] / mass)
        new_vel_ref[rows, :] = velocity
        new_disp_ref[rows, :] = disp_ref[rows, :] + time_step * velocity


def shape(*dims):
    return jax.ShapeDtypeStruct(dims, F32)


def shards(
    ref_pos,
    displacement,
    velocity,
    node_mass,
    elem_nodes,
    elem_part,
    elem_scale,
    part_stiff,
    shared,
    seg_node,
    seg_mask,
    send_blk,
    pair_a,
    pair_slot,
    pair_mask,
):
    axes = ("grp", "dev")
    peers, cap = send_blk.shape[1:]
    nodes = node_mass.shape[0]
    blocks, width = seg_node.shape
    elems = elem_nodes.shape[1]
    pairs = pair_a.shape[0]
    share = shared.shape[1]
    depth = nodes // WIDE
    slab = -(-(3 * cap + 1) // 8) * 8
    pos = ref_pos.reshape(3 * depth, WIDE)
    disp = displacement.reshape(3 * depth, WIDE)
    mass = node_mass.reshape(depth, WIDE)
    send = send_blk.reshape(-1)

    own, outgoing = pl.pallas_call(
        functools.partial(segment_kernel, cap),
        out_shape=(shape(blocks, 8, width), shape(peers, slab, width)),
        in_specs=[VMEM, VMEM, VMEM, VMEM, SMEM],
        out_specs=(VMEM, VMEM),
        compiler_params=PARAMS,
        name="segments",
    )(pos, disp, seg_node, seg_mask, send)
    arrived = lax.all_to_all(outgoing, axes, split_axis=0, concat_axis=0, tiled=True)

    chunk = math.gcd(elems, 512)
    force, ratio = pl.pallas_call(
        functools.partial(element_kernel, chunk),
        out_shape=(shape(3 * depth, WIDE), shape(8, width)),
        in_specs=[VMEM, VMEM, VMEM, VMEM, VMEM, SMEM],
        out_specs=(VMEM, VMEM),
        compiler_params=PARAMS,
        cost_estimate=pl.CostEstimate(
            flops=2 * 4 * elems * WIDE * depth * 18, bytes_accessed=2**20, transcendentals=0
        ),
        name="elements",
    )(disp, mass, elem_nodes, elem_part.reshape(1, -1), elem_scale.reshape(1, -1), part_stiff)

    group = math.gcd(pairs, 8)
    seg_force, going_back = pl.pallas_call(
        functools.partial(pair_kernel, cap, group),
        out_shape=(shape(blocks, 8, width), shape(peers, slab, width)),
        in_specs=[VMEM, VMEM, VMEM, SMEM, SMEM, SMEM],
        out_specs=(VMEM, VMEM),
        scratch_shapes=[
            pltpu.VMEM((blocks, width, 48), BF16),
            pltpu.VMEM((blocks, 32, 2 * width), BF16),
            pltpu.VMEM((peers * cap, 48, width), BF16),
            pltpu.VMEM((peers * cap, 32, 2 * width), BF16),
            pltpu.VMEM((blocks, 8, width), F32),
            pltpu.VMEM((peers * cap, 8, width), F32),
            pltpu.VMEM((cap, 8, width), F32),
        ],
        compiler_params=PARAMS,
        name="pairs",
    )(own, arrived, ratio, pair_a, pair_slot, pair_mask)
    returned = lax.all_to_all(going_back, axes, split_axis=0, concat_axis=0, tiled=True)

    piece = math.gcd(share, 1024)
    total, lower, upper, time_step = pl.pallas_call(
        functools.partial(total_kernel, cap, piece),
        out_shape=(shape(3 * depth, WIDE), shape(3, share), shape(3, share), shape(8, width)),
        in_specs=[VMEM, SMEM, VMEM, VMEM, VMEM, VMEM],
        out_specs=(VMEM, VMEM, VMEM, VMEM),
        scratch_shapes=[pltpu.VMEM((blocks, 8, width), F32)],
        compiler_params=PARAMS,
        name="totals",
    )(returned, send, seg_force, seg_node, force, shared)
    from_lower = shifted(lower, "dev", 1)
    from_upper = shifted(upper, "dev", -1)

    new_disp, new_vel = pl.pallas_call(
        functools.partial(update_kernel, piece),
        out_shape=(shape(3 * depth, WIDE), shape(3 * depth, WIDE)),
        in_specs=[VMEM] * 8,
        out_specs=(VMEM, VMEM),
        compiler_params=PARAMS,
        name="update",
    )(total, from_lower, from_upper, shared, mass, velocity.reshape(3 * depth, WIDE), disp, time_step)
    return (new_disp.reshape(3, nodes), new_vel.reshape(3, nodes))


def solution(mesh):
    return jax.shard_map(
        shards,
        mesh=mesh,
        in_specs=(
            P(None, ("grp", "dev")),
            P(None, ("grp", "dev")),
            P(None, ("grp", "dev")),
            P(("grp", "dev")),
            P(None, ("grp", "dev")),
            P(("grp", "dev")),
            P(("grp", "dev")),
            P(("grp", "dev")),
            P(None, ("grp", "dev")),
            P(("grp", "dev"), None),
            P(("grp", "dev"), None),
            P(("grp", "dev"), None, None),
            P(("grp", "dev")),
            P(("grp", "dev")),
            P(("grp", "dev")),
        ),
        out_specs=(P(None, ("grp", "dev")), P(None, ("grp", "dev"))),
        check_vma=False,
    )
```

```python
import functools
import math

import jax
import jax.numpy as jnp
from jax import lax
from jax.experimental import pallas as pl
from jax.experimental.pallas import tpu as pltpu
from jax.sharding import PartitionSpec as P

SPRINGS = ((0, 1, 1.0), (1, 2, 1.0), (2, 3, 1.0), (3, 0, 1.0), (0, 2, 0.5), (1, 3, 0.5))
COURANT = 0.5
LOG2E = 1.4426950408889634
FAR_AWAY = 64.0
WIDE = 256
LIMIT = 56 * 1024 * 1024
F32 = jnp.float32
BF16 = jnp.bfloat16
VMEM = pl.BlockSpec(memory_space=pltpu.VMEM)
SMEM = pl.BlockSpec(memory_space=pltpu.SMEM)
PARAMS = pltpu.CompilerParams(vmem_limit_bytes=LIMIT)


def shifted(value, axis, steps):
    count = lax.axis_size(axis)
    first, last = (max(0, -steps), min(count, count - steps))
    return lax.ppermute(value, axis, [(source, source + steps) for source in range(first, last)])


def split3(x):
    first = x.astype(BF16).astype(F32)
    rest = x - first
    second = rest.astype(BF16).astype(F32)
    third = (rest - second).astype(BF16).astype(F32)
    return first, second, third


def split_table(table):
    return jnp.concatenate(split3(table), 0).astype(BF16)


def selectors(index, depth):
    count = index.shape[1]
    low = index & (WIDE - 1)
    high = index // WIDE
    hot = jnp.where(lax.broadcasted_iota(jnp.int32, (WIDE, count), 0) == low, 1.0, 0.0)
    mask = lax.broadcasted_iota(jnp.int32, (depth, count), 0) == high
    return hot.astype(BF16), mask


def pick(table, hot, mask):
    depth = mask.shape[0]
    size = table.shape[0] // 3
    parts = jnp.dot(table, hot, preferred_element_type=F32)
    whole = parts[:size] + parts[size : 2 * size] + parts[2 * size :]
    return [
        jnp.sum(jnp.where(mask, whole[row : row + depth], 0.0), 0, keepdims=True)
        for row in range(0, size, depth)
    ]


def spread(rows, hot, mask):
    firsts, seconds = [], []
    for row in rows:
        first = row.astype(BF16).astype(F32)
        firsts.append(jnp.where(mask, first, 0.0))
        seconds.append(jnp.where(mask, row - first, 0.0))
    stacked = jnp.concatenate(firsts + seconds, 0).astype(BF16)
    sums = lax.dot_general(stacked, hot, (((1,), (1,)), ((), ())), preferred_element_type=F32)
    half = sums.shape[0] // 2
    return sums[:half] + sums[half:]


def lane_row(ref, start, count):
    tile = ref[pl.ds(pl.multiple_of(start, 8), count), :]
    return jnp.concatenate([tile[row : row + 1] for row in range(count)], 1)


def segment_kernel(cap, pos_ref, disp_ref, seg_ref, mask_ref, send_ref, own_ref, out_ref):
    depth = pos_ref.shape[0] // 3
    blocks, width = seg_ref.shape
    table = split_table(pos_ref[...] + disp_ref[...])

    def gather(step, carry):
        start = step * 8
        hot, mask = selectors(lane_row(seg_ref, start, 8), depth)
        live = lane_row(mask_ref, start, 8) > 0
        rows = [jnp.where(live, row, -FAR_AWAY) for row in pick(table, hot, mask)]
        square = rows[0] * rows[0] + rows[1] * rows[1] + rows[2] * rows[2]
        rows += [jnp.ones_like(square), -LOG2E * square]
        for block in range(8):
            lanes = slice(block * width, (block + 1) * width)
            for row in range(5):
                own_ref[start + block, row : row + 1, :] = rows[row][:, lanes]
            own_ref[start + block, 5:8, :] = jnp.zeros((3, width), F32)
        return carry

    lax.fori_loop(0, blocks // 8, gather, 0)

    def send(peer, carry):
        for slot in range(cap):
            block = own_ref[send_ref[peer * cap + slot], 0:3, :]
            out_ref[peer, 3 * slot : 3 * slot + 3, :] = jnp.where(
                block < -0.5 * FAR_AWAY, FAR_AWAY, block
            )
        out_ref[peer, 3 * cap :, :] = jnp.zeros((out_ref.shape[1] - 3 * cap, width), F32)
        return carry

    lax.fori_loop(0, out_ref.shape[0], send, 0)


def pull_kernel(
    chunk, disp_ref, mass_ref, nodes_ref, part_ref, scale_ref, stiff_ref, pull_ref, ratio_ref
):
    depth = mass_ref.shape[0]
    elems = nodes_ref.shape[1]
    parts = stiff_ref.shape[0]
    table = split_table(jnp.concatenate([disp_ref[...], mass_ref[...]], 0))

    def one_chunk(step, best):
        lanes = pl.ds(pl.multiple_of(step * chunk, chunk), chunk)
        local = lax.rem(part_ref[:, lanes], parts)
        stiff = jnp.zeros(local.shape, F32)
        for part in range(parts):
            stiff = jnp.where(local == part, stiff_ref[part], stiff)
        stiff = stiff * scale_ref[:, lanes]
        index = jnp.concatenate([nodes_ref[k : k + 1, lanes] for k in range(4)], 1)
        hot, mask = selectors(index, depth)
        rows = pick(table, hot, mask)
        corner = [[row[:, k * chunk : (k + 1) * chunk] for row in rows] for k in range(4)]
        mass = jnp.minimum(
            jnp.minimum(corner[0][3], corner[1][3]), jnp.minimum(corner[2][3], corner[3][3])
        )
        total = [[jnp.zeros_like(stiff) for axis in range(3)] for k in range(4)]
        for head, tail, weight in SPRINGS:
            for axis in range(3):
                pull = weight * stiff * (corner[tail][axis] - corner[head][axis])
                total[head][axis] = total[head][axis] + pull
                total[tail][axis] = total[tail][axis] - pull
        for axis in range(3):
            for k in range(4):
                pull_ref[4 * axis + k : 4 * axis + k + 1, lanes] = total[k][axis]
        return jnp.minimum(best, mass / stiff)

    best = lax.fori_loop(
        0, elems // chunk, one_chunk, jnp.full((1, chunk), jnp.inf, F32)
    )
    ratio_ref[...] = jnp.broadcast_to(jnp.min(best, 1, keepdims=True), ratio_ref.shape)


def force_kernel(chunk, pull_ref, nodes_ref, after_ref, force_ref):
    depth = force_ref.shape[0] // 3
    force_ref[...] = jnp.zeros_like(force_ref)

    def one_chunk(step, carry):
        lanes = pl.ds(pl.multiple_of(step * chunk, chunk), chunk)
        index = jnp.concatenate([nodes_ref[k : k + 1, lanes] for k in range(4)], 1)
        hot, mask = selectors(index, depth)
        rows = [
            jnp.concatenate([pull_ref[4 * axis + k : 4 * axis + k + 1, lanes] for k in range(4)], 1)
            for axis in range(3)
        ]
        force_ref[...] += spread(rows, hot, mask)
        return carry

    lax.fori_loop(0, nodes_ref.shape[1] // chunk, one_chunk, 0)


def pair_kernel(
    cap,
    group,
    own_ref,
    got_ref,
    ratio_ref,
    first_ref,
    second_ref,
    live_ref,
    seg_ref,
    back_ref,
    near_rows,
    near_turn,
    near_cols,
    far_rows,
    far_turn,
    far_cols,
    near_sum,
    far_sum,
    tile_ref,
):
    blocks, _, width = own_ref.shape
    peers = got_ref.shape[0]
    pairs = first_ref.shape[0]
    scale = 2.0 * LOG2E

    def doubled(parts):
        stacked = jnp.concatenate(parts + [jnp.zeros_like(parts[0])], 0)
        return jnp.concatenate([stacked, stacked], 1).astype(BF16)

    def prepare_near(step, carry):
        for member in range(8):
            block = 8 * step + member
            one, two, three = split3(own_ref[block])
            rows = jnp.concatenate([one, one, two, two, one, three], 0)
            near_rows[block] = rows.astype(BF16)
            near_turn[block] = rows.T.astype(BF16)
            near_cols[block] = doubled([one, two, three])
            near_sum[block] = jnp.zeros((8, width), F32)
        return carry

    lax.fori_loop(0, blocks // 8, prepare_near, 0)

    row_id = lax.broadcasted_iota(jnp.int32, (8, width), 0)
    tile_ref[...] = jnp.zeros_like(tile_ref)

    def prepare_far(peer, carry):
        for slot in range(cap):
            tile_ref[slot, 0:3, :] = got_ref[peer, 3 * slot : 3 * slot + 3, :]
        for slot in range(cap):
            tile = tile_ref[slot]
            square = -LOG2E * jnp.sum(tile * tile, 0, keepdims=True)
            one, two, three = split3(
                jnp.where(row_id == 3, square, jnp.where(row_id == 4, 1.0, scale * tile))
            )
            place = peer * cap + slot
            rows = jnp.concatenate([one, two, one, two, three, one], 0)
            far_rows[place] = rows.astype(BF16)
            far_turn[place] = rows.T.astype(BF16)
            far_cols[place] = doubled([one, two, three])
            far_sum[place] = jnp.zeros((8, width), F32)
        return carry

    lax.fori_loop(0, peers, prepare_far, 0)

    def weights(left, right):
        weight = jnp.exp2(jnp.dot(left, right, preferred_element_type=F32))
        first = weight.astype(BF16)
        second = (weight - first.astype(F32)).astype(BF16)
        return jnp.concatenate([first, second], 0)

    def one_group(step, carry):
        results = []
        for member in range(group):
            place = step * group + member
            near, far = first_ref[place], second_ref[place]
            live = live_ref[place].astype(F32)
            pushed = jnp.dot(
                far_cols[far], weights(far_turn[far], near_rows[near]), preferred_element_type=F32
            )
            recoil = jnp.dot(
                near_cols[near], weights(near_turn[near], far_rows[far]), preferred_element_type=F32
            )
            pushed = live * (pushed[0:8] + pushed[8:16] + pushed[16:24])
            recoil = live * (recoil[0:8] + recoil[8:16] + recoil[16:24])
            results.append((near, far, pushed, recoil))
        for near, far, pushed, recoil in results:
            near_sum[near] += pushed
            far_sum[far] += recoil
        return carry

    lax.fori_loop(0, pairs // group, one_group, 0)

    def finish_near(step, carry):
        for member in range(8):
            block = 8 * step + member
            sums = near_sum[block]
            seg_ref[block] = own_ref[block] * sums[4:5] - (1.0 / scale) * sums
        return carry

    lax.fori_loop(0, blocks // 8, finish_near, 0)

    def finish_far(peer, carry):
        for slot in range(cap):
            rows = slice(3 * slot, 3 * slot + 3)
            sums = far_sum[peer * cap + slot]
            back_ref[peer, rows, :] = got_ref[peer, rows, :] * sums[3:4] - sums[0:3]
        back_ref[peer, 3 * cap :, :] = jnp.broadcast_to(
            ratio_ref[0:1], (back_ref.shape[1] - 3 * cap, width)
        )
        return carry

    lax.fori_loop(0, peers, finish_far, 0)


def total_kernel(
    cap,
    chunk,
    back_ref,
    send_ref,
    own_ref,
    seg_ref,
    force_ref,
    shared_ref,
    total_ref,
    lower_ref,
    upper_ref,
    step_ref,
    sums,
):
    depth = force_ref.shape[0] // 3
    blocks, width = seg_ref.shape
    sums[...] = own_ref[...]

    def give_back(peer, best):
        for slot in range(cap):
            block = send_ref[peer * cap + slot]
            sums[block, 0:3, :] += back_ref[peer, 3 * slot : 3 * slot + 3, :]
        return jnp.minimum(best, back_ref[peer, 3 * cap : 3 * cap + 1, :])

    best = lax.fori_loop(
        0, back_ref.shape[0], give_back, jnp.full((1, width), jnp.inf, F32)
    )
    step_ref[...] = jnp.broadcast_to(COURANT * jnp.sqrt(best), step_ref.shape)
    total_ref[...] = force_ref[...]

    def scatter(step, carry):
        start = step * 8
        hot, mask = selectors(lane_row(seg_ref, start, 8), depth)
        rows = [
            jnp.concatenate([sums[start + block, row : row + 1, :] for block in range(8)], 1)
            for row in range(3)
        ]
        total_ref[...] += spread(rows, hot, mask)
        return carry

    lax.fori_loop(0, blocks // 8, scatter, 0)

    table = split_table(total_ref[...])

    def gather(step, carry):
        lanes = pl.ds(pl.multiple_of(step * chunk, chunk), chunk)
        for side, out_ref in ((0, upper_ref), (1, lower_ref)):
            hot, mask = selectors(shared_ref[side : side + 1, lanes], depth)
            rows = pick(table, hot, mask)
            for row in range(3):
                out_ref[row : row + 1, lanes] = rows[row]
        return carry

    lax.fori_loop(0, shared_ref.shape[1] // chunk, gather, 0)


def update_kernel(
    chunk,
    total_ref,
    lower_ref,
    upper_ref,
    shared_ref,
    mass_ref,
    vel_ref,
    disp_ref,
    step_ref,
    new_disp_ref,
    new_vel_ref,
):
    depth = mass_ref.shape[0]
    new_vel_ref[...] = total_ref[...]

    def scatter(step, carry):
        lanes = pl.ds(pl.multiple_of(step * chunk, chunk), chunk)
        for side, in_ref in ((0, lower_ref), (1, upper_ref)):
            hot, mask = selectors(shared_ref[side : side + 1, lanes], depth)
            rows = [in_ref[row : row + 1, lanes] for row in range(3)]
            new_vel_ref[...] += spread(rows, hot, mask)
        return carry

    lax.fori_loop(0, shared_ref.shape[1] // chunk, scatter, 0)
    time_step = step_ref[0:1, 0:1]
    mass = mass_ref[...]
    for axis in range(3):
        rows = slice(axis * depth, (axis + 1) * depth)
        velocity = vel_ref[rows, :] + time_step * (new_vel_ref[rows, :] / mass)
        new_vel_ref[rows, :] = velocity
        new_disp_ref[rows, :] = disp_ref[rows, :] + time_step * velocity


def shape(*dims):
    return jax.ShapeDtypeStruct(dims, F32)


def shards(
    ref_pos,
    displacement,
    velocity,
    node_mass,
    elem_nodes,
    elem_part,
    elem_scale,
    part_stiff,
    shared,
    seg_node,
    seg_mask,
    send_blk,
    pair_a,
    pair_slot,
    pair_mask,
):
    axes = ("grp", "dev")
    peers, cap = send_blk.shape[1:]
    nodes = node_mass.shape[0]
    blocks, width = seg_node.shape
    elems = elem_nodes.shape[1]
    pairs = pair_a.shape[0]
    share = shared.shape[1]
    depth = nodes // WIDE
    slab = -(-(3 * cap + 1) // 8) * 8
    pos = ref_pos.reshape(3 * depth, WIDE)
    disp = displacement.reshape(3 * depth, WIDE)
    mass = node_mass.reshape(depth, WIDE)
    send = send_blk.reshape(-1)

    own, outgoing = pl.pallas_call(
        functools.partial(segment_kernel, cap),
        out_shape=(shape(blocks, 8, width), shape(peers, slab, width)),
        in_specs=[VMEM, VMEM, VMEM, VMEM, SMEM],
        out_specs=(VMEM, VMEM),
        compiler_params=PARAMS,
        name="segments",
    )(pos, disp, seg_node, seg_mask, send)
    arrived = lax.all_to_all(outgoing, axes, split_axis=0, concat_axis=0, tiled=True)

    chunk = math.gcd(elems, 512)
    work = 2 * 4 * elems * WIDE * depth
    pull, ratio = pl.pallas_call(
        functools.partial(pull_kernel, chunk),
        out_shape=(shape(12, elems), shape(8, width)),
        in_specs=[VMEM, VMEM, VMEM, VMEM, VMEM, SMEM],
        out_specs=(VMEM, VMEM),
        compiler_params=PARAMS,
        cost_estimate=pl.CostEstimate(flops=12 * work, bytes_accessed=2**20, transcendentals=0),
        name="pulls",
    )(disp, mass, elem_nodes, elem_part.reshape(1, -1), elem_scale.reshape(1, -1), part_stiff)

    group = math.gcd(pairs, 8)
    seg_force, going_back = pl.pallas_call(
        functools.partial(pair_kernel, cap, group),
        out_shape=(shape(blocks, 8, width), shape(peers, slab, width)),
        in_specs=[VMEM, VMEM, VMEM, SMEM, SMEM, SMEM],
        out_specs=(VMEM, VMEM),
        scratch_shapes=[
            pltpu.VMEM((blocks, 48, width), BF16),
            pltpu.VMEM((blocks, width, 48), BF16),
            pltpu.VMEM((blocks, 32, 2 * width), BF16),
            pltpu.VMEM((peers * cap, 48, width), BF16),
            pltpu.VMEM((peers * cap, width, 48), BF16),
            pltpu.VMEM((peers * cap, 32, 2 * width), BF16),
            pltpu.VMEM((blocks, 8, width), F32),
            pltpu.VMEM((peers * cap, 8, width), F32),
            pltpu.VMEM((cap, 8, width), F32),
        ],
        compiler_params=PARAMS,
        name="pairs",
    )(own, arrived, ratio, pair_a, pair_slot, pair_mask)
    returned = lax.all_to_all(going_back, axes, split_axis=0, concat_axis=0, tiled=True)

    force = pl.pallas_call(
        functools.partial(force_kernel, chunk),
        out_shape=shape(3 * depth, WIDE),
        in_specs=[VMEM, VMEM, pl.BlockSpec(memory_space=pl.ANY)],
        out_specs=VMEM,
        compiler_params=PARAMS,
        cost_estimate=pl.CostEstimate(flops=12 * work, bytes_accessed=2**20, transcendentals=0),
        name="forces",
    )(pull, elem_nodes, seg_force)

    piece = math.gcd(share, 1024)
    total, lower, upper, time_step = pl.pallas_call(
        functools.partial(total_kernel, cap, piece),
        out_shape=(shape(3 * depth, WIDE), shape(3, share), shape(3, share), shape(8, width)),
        in_specs=[VMEM, SMEM, VMEM, VMEM, VMEM, VMEM],
        out_specs=(VMEM, VMEM, VMEM, VMEM),
        scratch_shapes=[pltpu.VMEM((blocks, 8, width), F32)],
        compiler_params=PARAMS,
        name="totals",
    )(returned, send, seg_force, seg_node, force, shared)
    from_lower = shifted(lower, "dev", 1)
    from_upper = shifted(upper, "dev", -1)

    new_disp, new_vel = pl.pallas_call(
        functools.partial(update_kernel, piece),
        out_shape=(shape(3 * depth, WIDE), shape(3 * depth, WIDE)),
        in_specs=[VMEM] * 8,
        out_specs=(VMEM, VMEM),
        compiler_params=PARAMS,
        name="update",
    )(total, from_lower, from_upper, shared, mass, velocity.reshape(3 * depth, WIDE), disp, time_step)
    return (new_disp.reshape(3, nodes), new_vel.reshape(3, nodes))


def solution(mesh):
    return jax.shard_map(
        shards,
        mesh=mesh,
        in_specs=(
            P(None, ("grp", "dev")),
            P(None, ("grp", "dev")),
            P(None, ("grp", "dev")),
            P(("grp", "dev")),
            P(None, ("grp", "dev")),
            P(("grp", "dev")),
            P(("grp", "dev")),
            P(("grp", "dev")),
            P(None, ("grp", "dev")),
            P(("grp", "dev"), None),
            P(("grp", "dev"), None),
            P(("grp", "dev"), None, None),
            P(("grp", "dev")),
            P(("grp", "dev")),
            P(("grp", "dev")),
        ),
        out_specs=(P(None, ("grp", "dev")), P(None, ("grp", "dev"))),
        check_vma=False,
    )
```

```python
import functools
import math

import jax
import jax.numpy as jnp
from jax import lax
from jax.experimental import pallas as pl
from jax.experimental.pallas import tpu as pltpu
from jax.sharding import PartitionSpec as P

SPRINGS = ((0, 1, 1.0), (1, 2, 1.0), (2, 3, 1.0), (3, 0, 1.0), (0, 2, 0.5), (1, 3, 0.5))
COURANT = 0.5
LOG2E = 1.4426950408889634
FAR_AWAY = 64.0
WIDE = 256
LIMIT = 56 * 1024 * 1024
F32 = jnp.float32
BF16 = jnp.bfloat16
VMEM = pl.BlockSpec(memory_space=pltpu.VMEM)
SMEM = pl.BlockSpec(memory_space=pltpu.SMEM)
PARAMS = pltpu.CompilerParams(vmem_limit_bytes=LIMIT)


def shifted(value, axis, steps):
    count = lax.axis_size(axis)
    first, last = (max(0, -steps), min(count, count - steps))
    return lax.ppermute(value, axis, [(source, source + steps) for source in range(first, last)])


def split3(x):
    first = x.astype(BF16).astype(F32)
    rest = x - first
    second = rest.astype(BF16).astype(F32)
    third = (rest - second).astype(BF16).astype(F32)
    return first, second, third


def split_table(table):
    return jnp.concatenate(split3(table), 0).astype(BF16)


def selectors(index, depth):
    count = index.shape[1]
    low = index & (WIDE - 1)
    high = index // WIDE
    hot = jnp.where(lax.broadcasted_iota(jnp.int32, (WIDE, count), 0) == low, 1.0, 0.0)
    mask = lax.broadcasted_iota(jnp.int32, (depth, count), 0) == high
    return hot.astype(BF16), mask


def pick(table, hot, mask):
    depth = mask.shape[0]
    size = table.shape[0] // 3
    parts = jnp.dot(table, hot, preferred_element_type=F32)
    whole = parts[:size] + parts[size : 2 * size] + parts[2 * size :]
    return [
        jnp.sum(jnp.where(mask, whole[row : row + depth], 0.0), 0, keepdims=True)
        for row in range(0, size, depth)
    ]


def spread(rows, hot, mask):
    firsts, seconds = [], []
    for row in rows:
        first = row.astype(BF16).astype(F32)
        firsts.append(jnp.where(mask, first, 0.0))
        seconds.append(jnp.where(mask, row - first, 0.0))
    stacked = jnp.concatenate(firsts + seconds, 0).astype(BF16)
    sums = lax.dot_general(stacked, hot, (((1,), (1,)), ((), ())), preferred_element_type=F32)
    half = sums.shape[0] // 2
    return sums[:half] + sums[half:]


def fold(ref, to_ref, first=0):
    rows, nodes = ref.shape
    depth = nodes // WIDE
    for row in range(rows):
        for high in range(depth):
            place = first + row * depth + high
            to_ref[place : place + 1, :] = ref[row : row + 1, high * WIDE : (high + 1) * WIDE]


def unfold(ref, to_ref):
    rows, nodes = to_ref.shape
    depth = nodes // WIDE
    for row in range(rows):
        for high in range(depth):
            place = row * depth + high
            to_ref[row : row + 1, high * WIDE : (high + 1) * WIDE] = ref[place : place + 1, :]


def lane_row(ref, start, count):
    tile = ref[pl.ds(pl.multiple_of(start, 8), count), :]
    return jnp.concatenate([tile[row : row + 1] for row in range(count)], 1)


def segment_kernel(
    cap, pos_ref, disp_ref, seg_ref, mask_ref, send_ref, own_ref, out_ref, table_ref, moved_ref
):
    depth = table_ref.shape[0] // 3
    blocks, width = seg_ref.shape
    moved_ref[...] = pos_ref[...] + disp_ref[...]
    fold(moved_ref, table_ref)
    table = split_table(table_ref[...])

    def gather(step, carry):
        start = step * 8
        hot, mask = selectors(lane_row(seg_ref, start, 8), depth)
        live = lane_row(mask_ref, start, 8) > 0
        rows = [jnp.where(live, row, -FAR_AWAY) for row in pick(table, hot, mask)]
        square = rows[0] * rows[0] + rows[1] * rows[1] + rows[2] * rows[2]
        rows += [jnp.ones_like(square), -LOG2E * square]
        for block in range(8):
            lanes = slice(block * width, (block + 1) * width)
            for row in range(5):
                own_ref[start + block, row : row + 1, :] = rows[row][:, lanes]
            own_ref[start + block, 5:8, :] = jnp.zeros((3, width), F32)
        return carry

    lax.fori_loop(0, blocks // 8, gather, 0)

    def send(peer, carry):
        for slot in range(cap):
            block = own_ref[send_ref[0, peer, slot], 0:3, :]
            out_ref[peer, 3 * slot : 3 * slot + 3, :] = jnp.where(
                block < -0.5 * FAR_AWAY, FAR_AWAY, block
            )
        out_ref[peer, 3 * cap :, :] = jnp.zeros((out_ref.shape[1] - 3 * cap, width), F32)
        return carry

    lax.fori_loop(0, out_ref.shape[0], send, 0)


def pull_kernel(
    chunk, disp_ref, mass_ref, nodes_ref, part_ref, scale_ref, stiff_ref, pull_ref, ratio_ref, table_ref
):
    depth = table_ref.shape[0] // 4
    elems = nodes_ref.shape[1]
    parts = stiff_ref.shape[0]
    fold(disp_ref, table_ref)
    fold(mass_ref, table_ref, 3 * depth)
    table = split_table(table_ref[...])

    def one_chunk(step, best):
        lanes = pl.ds(pl.multiple_of(step * chunk, chunk), chunk)
        local = lax.rem(part_ref[:, lanes], parts)
        stiff = jnp.zeros(local.shape, F32)
        for part in range(parts):
            stiff = jnp.where(local == part, stiff_ref[part], stiff)
        stiff = stiff * scale_ref[:, lanes]
        index = jnp.concatenate([nodes_ref[k : k + 1, lanes] for k in range(4)], 1)
        hot, mask = selectors(index, depth)
        rows = pick(table, hot, mask)
        corner = [[row[:, k * chunk : (k + 1) * chunk] for row in rows] for k in range(4)]
        mass = jnp.minimum(
            jnp.minimum(corner[0][3], corner[1][3]), jnp.minimum(corner[2][3], corner[3][3])
        )
        total = [[jnp.zeros_like(stiff) for axis in range(3)] for k in range(4)]
        for head, tail, weight in SPRINGS:
            for axis in range(3):
                pull = weight * stiff * (corner[tail][axis] - corner[head][axis])
                total[head][axis] = total[head][axis] + pull
                total[tail][axis] = total[tail][axis] - pull
        for axis in range(3):
            for k in range(4):
                pull_ref[4 * axis + k : 4 * axis + k + 1, lanes] = total[k][axis]
        return jnp.minimum(best, mass / stiff)

    best = lax.fori_loop(
        0, elems // chunk, one_chunk, jnp.full((1, chunk), jnp.inf, F32)
    )
    ratio_ref[...] = jnp.broadcast_to(jnp.min(best, 1, keepdims=True), ratio_ref.shape)


def force_kernel(chunk, pull_ref, nodes_ref, after_ref, force_ref):
    depth = force_ref.shape[0] // 3
    force_ref[...] = jnp.zeros_like(force_ref)

    def one_chunk(step, carry):
        lanes = pl.ds(pl.multiple_of(step * chunk, chunk), chunk)
        index = jnp.concatenate([nodes_ref[k : k + 1, lanes] for k in range(4)], 1)
        hot, mask = selectors(index, depth)
        rows = [
            jnp.concatenate([pull_ref[4 * axis + k : 4 * axis + k + 1, lanes] for k in range(4)], 1)
            for axis in range(3)
        ]
        force_ref[...] += spread(rows, hot, mask)
        return carry

    lax.fori_loop(0, nodes_ref.shape[1] // chunk, one_chunk, 0)


def pair_kernel(
    cap,
    group,
    own_ref,
    got_ref,
    ratio_ref,
    first_ref,
    second_ref,
    live_ref,
    seg_ref,
    back_ref,
    near_rows,
    near_turn,
    near_cols,
    far_rows,
    far_turn,
    far_cols,
    near_sum,
    far_sum,
    tile_ref,
):
    blocks, _, width = own_ref.shape
    peers = got_ref.shape[0]
    pairs = first_ref.shape[0]
    scale = 2.0 * LOG2E

    row_id = lax.broadcasted_iota(jnp.int32, (8, width), 0)
    pad = jnp.zeros((16, width), BF16)
    gap = jnp.zeros((64, width), BF16)

    def operands(tile):
        one, two, three = split3(tile)
        mixed = jnp.where(row_id < 3, two, pltpu.roll(three, 3, 0))
        mixed = jnp.where(row_id < 6, mixed, 0.0)
        columns = jnp.concatenate([one, mixed], 0)
        return one, two, three, jnp.concatenate([columns, columns], 1).astype(BF16)

    def prepare_near(step, carry):
        for member in range(8):
            block = 8 * step + member
            one, two, three, columns = operands(own_ref[block])
            rows = jnp.concatenate([one, one, two, two, one, three], 0).astype(BF16)
            rows = jnp.concatenate([rows, pad], 0)
            near_rows[block] = rows
            near_turn[block] = jnp.concatenate([rows, gap], 0).T
            near_cols[block] = columns
            near_sum[block] = jnp.zeros((16, width), F32)
        return carry

    lax.fori_loop(0, blocks // 8, prepare_near, 0)

    tile_ref[...] = jnp.zeros_like(tile_ref)

    def prepare_far(peer, carry):
        for slot in range(cap):
            tile_ref[slot, 0:3, :] = got_ref[peer, 3 * slot : 3 * slot + 3, :]
        for slot in range(cap):
            tile = tile_ref[slot]
            square = -LOG2E * jnp.sum(tile * tile, 0, keepdims=True)
            one, two, three, columns = operands(
                jnp.where(row_id == 3, square, jnp.where(row_id == 4, 1.0, scale * tile))
            )
            place = peer * cap + slot
            rows = jnp.concatenate([one, two, one, two, three, one], 0).astype(BF16)
            rows = jnp.concatenate([rows, pad], 0)
            far_rows[place] = rows
            far_turn[place] = jnp.concatenate([gap, rows], 0).T
            far_cols[place] = columns
            far_sum[place] = jnp.zeros((16, width), F32)
        return carry

    lax.fori_loop(0, peers, prepare_far, 0)

    def one_group(step, carry):
        results = []
        for member in range(group):
            place = step * group + member
            near, far = first_ref[place], second_ref[place]
            live = live_ref[place].astype(F32)
            right = jnp.concatenate(
                [
                    jnp.concatenate([far_rows[far], gap], 1),
                    jnp.concatenate([gap, near_rows[near]], 1),
                ],
                0,
            )
            both = jnp.dot(
                near_turn[near] + far_turn[far], right, preferred_element_type=F32
            )
            weight = jnp.exp2(both)
            first = weight.astype(BF16)
            second = (weight - first.astype(F32)).astype(BF16)
            sums = jnp.dot(
                jnp.concatenate([near_cols[near], far_cols[far]], 0),
                jnp.concatenate([first, second], 0),
                preferred_element_type=F32,
            )
            results.append((near, far, live * sums[16:, width:], live * sums[:16, :width]))
        for near, far, pushed, recoil in results:
            near_sum[near] += pushed
            far_sum[far] += recoil
        return carry

    lax.fori_loop(0, pairs // group, one_group, 0)

    def joined(sums):
        low = sums[8:16]
        return sums[:8] + jnp.where(row_id < 3, low + pltpu.roll(low, 5, 0), 0.0)

    def finish_near(step, carry):
        for member in range(8):
            block = 8 * step + member
            sums = joined(near_sum[block])
            seg_ref[block] = own_ref[block] * sums[4:5] - (1.0 / scale) * sums
        return carry

    lax.fori_loop(0, blocks // 8, finish_near, 0)

    def finish_far(peer, carry):
        for slot in range(cap):
            rows = slice(3 * slot, 3 * slot + 3)
            sums = joined(far_sum[peer * cap + slot])
            back_ref[peer, rows, :] = got_ref[peer, rows, :] * sums[3:4] - sums[0:3]
        back_ref[peer, 3 * cap :, :] = jnp.broadcast_to(
            ratio_ref[0:1], (back_ref.shape[1] - 3 * cap, width)
        )
        return carry

    lax.fori_loop(0, peers, finish_far, 0)


def total_kernel(
    cap,
    chunk,
    back_ref,
    send_ref,
    own_ref,
    seg_ref,
    force_ref,
    shared_ref,
    total_ref,
    lower_ref,
    upper_ref,
    step_ref,
    sums,
):
    depth = force_ref.shape[0] // 3
    blocks, width = seg_ref.shape
    sums[...] = own_ref[...]

    def give_back(peer, best):
        for slot in range(cap):
            block = send_ref[0, peer, slot]
            sums[block, 0:3, :] += back_ref[peer, 3 * slot : 3 * slot + 3, :]
        return jnp.minimum(best, back_ref[peer, 3 * cap : 3 * cap + 1, :])

    best = lax.fori_loop(
        0, back_ref.shape[0], give_back, jnp.full((1, width), jnp.inf, F32)
    )
    step_ref[...] = jnp.broadcast_to(COURANT * jnp.sqrt(best), step_ref.shape)
    total_ref[...] = force_ref[...]

    def scatter(step, carry):
        start = step * 8
        hot, mask = selectors(lane_row(seg_ref, start, 8), depth)
        rows = [
            jnp.concatenate([sums[start + block, row : row + 1, :] for block in range(8)], 1)
            for row in range(3)
        ]
        total_ref[...] += spread(rows, hot, mask)
        return carry

    lax.fori_loop(0, blocks // 8, scatter, 0)

    table = split_table(total_ref[...])

    def gather(step, carry):
        lanes = pl.ds(pl.multiple_of(step * chunk, chunk), chunk)
        for side, out_ref in ((0, upper_ref), (1, lower_ref)):
            hot, mask = selectors(shared_ref[side : side + 1, lanes], depth)
            rows = pick(table, hot, mask)
            for row in range(3):
                out_ref[row : row + 1, lanes] = rows[row]
        return carry

    lax.fori_loop(0, shared_ref.shape[1] // chunk, gather, 0)


def update_kernel(
    chunk,
    total_ref,
    lower_ref,
    upper_ref,
    shared_ref,
    mass_ref,
    vel_ref,
    disp_ref,
    step_ref,
    new_disp_ref,
    new_vel_ref,
    sums,
):
    sums[...] = total_ref[...]
    depth = sums.shape[0] // 3

    def scatter(step, carry):
        lanes = pl.ds(pl.multiple_of(step * chunk, chunk), chunk)
        for side, in_ref in ((0, lower_ref), (1, upper_ref)):
            hot, mask = selectors(shared_ref[side : side + 1, lanes], depth)
            rows = [in_ref[row : row + 1, lanes] for row in range(3)]
            sums[...] += spread(rows, hot, mask)
        return carry

    lax.fori_loop(0, shared_ref.shape[1] // chunk, scatter, 0)
    unfold(sums, new_vel_ref)
    time_step = step_ref[0:1, 0:1]
    velocity = vel_ref[...] + time_step * (new_vel_ref[...] / mass_ref[...])
    new_vel_ref[...] = velocity
    new_disp_ref[...] = disp_ref[...] + time_step * velocity


def shape(*dims):
    return jax.ShapeDtypeStruct(dims, F32)


def shards(
    ref_pos,
    displacement,
    velocity,
    node_mass,
    elem_nodes,
    elem_part,
    elem_scale,
    part_stiff,
    shared,
    seg_node,
    seg_mask,
    send_blk,
    pair_a,
    pair_slot,
    pair_mask,
):
    axes = ("grp", "dev")
    peers, cap = send_blk.shape[1:]
    nodes = node_mass.shape[0]
    blocks, width = seg_node.shape
    elems = elem_nodes.shape[1]
    pairs = pair_a.shape[0]
    share = shared.shape[1]
    depth = nodes // WIDE
    slab = -(-(3 * cap + 1) // 8) * 8
    mass = node_mass.reshape(1, -1)

    own, outgoing = pl.pallas_call(
        functools.partial(segment_kernel, cap),
        out_shape=(shape(blocks, 8, width), shape(peers, slab, width)),
        in_specs=[VMEM, VMEM, VMEM, VMEM, SMEM],
        out_specs=(VMEM, VMEM),
        scratch_shapes=[pltpu.VMEM((3 * depth, WIDE), F32), pltpu.VMEM((3, nodes), F32)],
        compiler_params=PARAMS,
        name="segments",
    )(ref_pos, displacement, seg_node, seg_mask, send_blk)
    arrived = lax.all_to_all(outgoing, axes, split_axis=0, concat_axis=0, tiled=True)

    chunk = math.gcd(elems, 512)
    work = 2 * 4 * elems * WIDE * depth
    pull, ratio = pl.pallas_call(
        functools.partial(pull_kernel, chunk),
        out_shape=(shape(12, elems), shape(8, width)),
        in_specs=[VMEM, VMEM, VMEM, VMEM, VMEM, SMEM],
        out_specs=(VMEM, VMEM),
        scratch_shapes=[pltpu.VMEM((4 * depth, WIDE), F32)],
        compiler_params=PARAMS,
        cost_estimate=pl.CostEstimate(flops=12 * work, bytes_accessed=2**20, transcendentals=0),
        name="pulls",
    )(displacement, mass, elem_nodes, elem_part.reshape(1, -1), elem_scale.reshape(1, -1), part_stiff)

    group = math.gcd(pairs, 8)
    seg_force, going_back = pl.pallas_call(
        functools.partial(pair_kernel, cap, group),
        out_shape=(shape(blocks, 8, width), shape(peers, slab, width)),
        in_specs=[VMEM, VMEM, VMEM, SMEM, SMEM, SMEM],
        out_specs=(VMEM, VMEM),
        scratch_shapes=[
            pltpu.VMEM((blocks, 64, width), BF16),
            pltpu.VMEM((blocks, width, width), BF16),
            pltpu.VMEM((blocks, 16, 2 * width), BF16),
            pltpu.VMEM((peers * cap, 64, width), BF16),
            pltpu.VMEM((peers * cap, width, width), BF16),
            pltpu.VMEM((peers * cap, 16, 2 * width), BF16),
            pltpu.VMEM((blocks, 16, width), F32),
            pltpu.VMEM((peers * cap, 16, width), F32),
            pltpu.VMEM((cap, 8, width), F32),
        ],
        compiler_params=PARAMS,
        name="pairs",
    )(own, arrived, ratio, pair_a, pair_slot, pair_mask)
    returned = lax.all_to_all(going_back, axes, split_axis=0, concat_axis=0, tiled=True)

    force = pl.pallas_call(
        functools.partial(force_kernel, chunk),
        out_shape=shape(3 * depth, WIDE),
        in_specs=[VMEM, VMEM, pl.BlockSpec(memory_space=pl.ANY)],
        out_specs=VMEM,
        compiler_params=PARAMS,
        cost_estimate=pl.CostEstimate(flops=12 * work, bytes_accessed=2**20, transcendentals=0),
        name="forces",
    )(pull, elem_nodes, seg_force)

    piece = math.gcd(share, 1024)
    total, lower, upper, time_step = pl.pallas_call(
        functools.partial(total_kernel, cap, piece),
        out_shape=(shape(3 * depth, WIDE), shape(3, share), shape(3, share), shape(8, width)),
        in_specs=[VMEM, SMEM, VMEM, VMEM, VMEM, VMEM],
        out_specs=(VMEM, VMEM, VMEM, VMEM),
        scratch_shapes=[pltpu.VMEM((blocks, 8, width), F32)],
        compiler_params=PARAMS,
        name="totals",
    )(returned, send_blk, seg_force, seg_node, force, shared)
    from_lower = shifted(lower, "dev", 1)
    from_upper = shifted(upper, "dev", -1)

    return pl.pallas_call(
        functools.partial(update_kernel, piece),
        out_shape=(shape(3, nodes), shape(3, nodes)),
        in_specs=[VMEM] * 8,
        out_specs=(VMEM, VMEM),
        scratch_shapes=[pltpu.VMEM((3 * depth, WIDE), F32)],
        compiler_params=PARAMS,
        name="update",
    )(total, from_lower, from_upper, shared, mass, velocity, displacement, time_step)


def solution(mesh):
    return jax.shard_map(
        shards,
        mesh=mesh,
        in_specs=(
            P(None, ("grp", "dev")),
            P(None, ("grp", "dev")),
            P(None, ("grp", "dev")),
            P(("grp", "dev")),
            P(None, ("grp", "dev")),
            P(("grp", "dev")),
            P(("grp", "dev")),
            P(("grp", "dev")),
            P(None, ("grp", "dev")),
            P(("grp", "dev"), None),
            P(("grp", "dev"), None),
            P(("grp", "dev"), None, None),
            P(("grp", "dev")),
            P(("grp", "dev")),
            P(("grp", "dev")),
        ),
        out_specs=(P(None, ("grp", "dev")), P(None, ("grp", "dev"))),
        check_vma=False,
    )
```

```python
import functools
import math

import jax
import jax.numpy as jnp
from jax import lax
from jax.experimental import pallas as pl
from jax.experimental.pallas import tpu as pltpu
from jax.sharding import PartitionSpec as P

SPRINGS = ((0, 1, 1.0), (1, 2, 1.0), (2, 3, 1.0), (3, 0, 1.0), (0, 2, 0.5), (1, 3, 0.5))
COURANT = 0.5
LOG2E = 1.4426950408889634
FAR_AWAY = 64.0
WIDE = 256
LIMIT = 56 * 1024 * 1024
F32 = jnp.float32
BF16 = jnp.bfloat16
VMEM = pl.BlockSpec(memory_space=pltpu.VMEM)
SMEM = pl.BlockSpec(memory_space=pltpu.SMEM)
PARAMS = pltpu.CompilerParams(vmem_limit_bytes=LIMIT)


def shifted(value, axis, steps):
    count = lax.axis_size(axis)
    first, last = (max(0, -steps), min(count, count - steps))
    return lax.ppermute(value, axis, [(source, source + steps) for source in range(first, last)])


def split3(x):
    first = x.astype(BF16).astype(F32)
    rest = x - first
    second = rest.astype(BF16).astype(F32)
    third = (rest - second).astype(BF16).astype(F32)
    return first, second, third


def split_table(table):
    return jnp.concatenate(split3(table), 0).astype(BF16)


def selectors(index, depth):
    count = index.shape[1]
    low = index & (WIDE - 1)
    high = index // WIDE
    hot = jnp.where(lax.broadcasted_iota(jnp.int32, (WIDE, count), 0) == low, 1.0, 0.0)
    mask = lax.broadcasted_iota(jnp.int32, (depth, count), 0) == high
    return hot.astype(BF16), mask


def pick(table, hot, mask):
    depth = mask.shape[0]
    size = table.shape[0] // 3
    parts = jnp.dot(table, hot, preferred_element_type=F32)
    whole = parts[:size] + parts[size : 2 * size] + parts[2 * size :]
    return [
        jnp.sum(jnp.where(mask, whole[row : row + depth], 0.0), 0, keepdims=True)
        for row in range(0, size, depth)
    ]


def spread(rows, hot, mask):
    firsts, seconds = [], []
    for row in rows:
        first = row.astype(BF16).astype(F32)
        firsts.append(jnp.where(mask, first, 0.0))
        seconds.append(jnp.where(mask, row - first, 0.0))
    stacked = jnp.concatenate(firsts + seconds, 0).astype(BF16)
    sums = lax.dot_general(stacked, hot, (((1,), (1,)), ((), ())), preferred_element_type=F32)
    half = sums.shape[0] // 2
    return sums[:half] + sums[half:]


def fold(ref, to_ref, first=0):
    rows, nodes = ref.shape
    depth = nodes // WIDE
    for row in range(rows):
        for high in range(depth):
            place = first + row * depth + high
            to_ref[place : place + 1, :] = ref[row : row + 1, high * WIDE : (high + 1) * WIDE]


def unfold(ref, to_ref):
    rows, nodes = to_ref.shape
    depth = nodes // WIDE
    for row in range(rows):
        for high in range(depth):
            place = row * depth + high
            to_ref[row : row + 1, high * WIDE : (high + 1) * WIDE] = ref[place : place + 1, :]


def lane_row(ref, start, count):
    tile = ref[pl.ds(pl.multiple_of(start, 8), count), :]
    return jnp.concatenate([tile[row : row + 1] for row in range(count)], 1)


def segment_kernel(
    cap, pos_ref, disp_ref, seg_ref, mask_ref, send_ref, own_ref, out_ref, table_ref, moved_ref
):
    depth = table_ref.shape[0] // 3
    blocks, width = seg_ref.shape
    moved_ref[...] = pos_ref[...] + disp_ref[...]
    fold(moved_ref, table_ref)
    table = split_table(table_ref[...])

    def gather(step, carry):
        start = step * 8
        hot, mask = selectors(lane_row(seg_ref, start, 8), depth)
        live = lane_row(mask_ref, start, 8) > 0
        rows = [jnp.where(live, row, -FAR_AWAY) for row in pick(table, hot, mask)]
        square = rows[0] * rows[0] + rows[1] * rows[1] + rows[2] * rows[2]
        rows += [jnp.ones_like(square), -LOG2E * square]
        for block in range(8):
            lanes = slice(block * width, (block + 1) * width)
            for row in range(5):
                own_ref[start + block, row : row + 1, :] = rows[row][:, lanes]
            own_ref[start + block, 5:8, :] = jnp.zeros((3, width), F32)
        return carry

    lax.fori_loop(0, blocks // 8, gather, 0)

    def send(peer, carry):
        for slot in range(cap):
            block = own_ref[send_ref[0, peer, slot], 0:3, :]
            out_ref[peer, 3 * slot : 3 * slot + 3, :] = jnp.where(
                block < -0.5 * FAR_AWAY, FAR_AWAY, block
            )
        out_ref[peer, 3 * cap :, :] = jnp.zeros((out_ref.shape[1] - 3 * cap, width), F32)
        return carry

    lax.fori_loop(0, out_ref.shape[0], send, 0)


def pull_kernel(
    chunk, disp_ref, mass_ref, nodes_ref, part_ref, scale_ref, stiff_ref, pull_ref, ratio_ref, table_ref
):
    depth = table_ref.shape[0] // 4
    elems = nodes_ref.shape[1]
    parts = stiff_ref.shape[0]
    fold(disp_ref, table_ref)
    fold(mass_ref, table_ref, 3 * depth)
    table = split_table(table_ref[...])

    def one_chunk(step, best):
        lanes = pl.ds(pl.multiple_of(step * chunk, chunk), chunk)
        local = lax.rem(part_ref[:, lanes], parts)
        stiff = jnp.zeros(local.shape, F32)
        for part in range(parts):
            stiff = jnp.where(local == part, stiff_ref[part], stiff)
        stiff = stiff * scale_ref[:, lanes]
        index = jnp.concatenate([nodes_ref[k : k + 1, lanes] for k in range(4)], 1)
        hot, mask = selectors(index, depth)
        rows = pick(table, hot, mask)
        corner = [[row[:, k * chunk : (k + 1) * chunk] for row in rows] for k in range(4)]
        mass = jnp.minimum(
            jnp.minimum(corner[0][3], corner[1][3]), jnp.minimum(corner[2][3], corner[3][3])
        )
        total = [[jnp.zeros_like(stiff) for axis in range(3)] for k in range(4)]
        for head, tail, weight in SPRINGS:
            for axis in range(3):
                pull = weight * stiff * (corner[tail][axis] - corner[head][axis])
                total[head][axis] = total[head][axis] + pull
                total[tail][axis] = total[tail][axis] - pull
        for axis in range(3):
            for k in range(4):
                pull_ref[4 * axis + k : 4 * axis + k + 1, lanes] = total[k][axis]
        return jnp.minimum(best, mass / stiff)

    best = lax.fori_loop(
        0, elems // chunk, one_chunk, jnp.full((1, chunk), jnp.inf, F32)
    )
    ratio_ref[...] = jnp.broadcast_to(jnp.min(best, 1, keepdims=True), ratio_ref.shape)


def force_kernel(chunk, pull_ref, nodes_ref, after_ref, force_ref):
    depth = force_ref.shape[0] // 3
    force_ref[...] = jnp.zeros_like(force_ref)

    def one_chunk(step, carry):
        lanes = pl.ds(pl.multiple_of(step * chunk, chunk), chunk)
        index = jnp.concatenate([nodes_ref[k : k + 1, lanes] for k in range(4)], 1)
        hot, mask = selectors(index, depth)
        rows = [
            jnp.concatenate([pull_ref[4 * axis + k : 4 * axis + k + 1, lanes] for k in range(4)], 1)
            for axis in range(3)
        ]
        force_ref[...] += spread(rows, hot, mask)
        return carry

    lax.fori_loop(0, nodes_ref.shape[1] // chunk, one_chunk, 0)


def pair_kernel(
    cap,
    group,
    own_ref,
    got_ref,
    ratio_ref,
    first_ref,
    second_ref,
    live_ref,
    seg_ref,
    back_ref,
    near_turn,
    near_cols,
    far_rows,
    far_turn,
    near_sum,
    far_sum,
    tile_ref,
):
    blocks, _, width = own_ref.shape
    peers = got_ref.shape[0]
    pairs = first_ref.shape[0]
    scale = 2.0 * LOG2E

    row_id = lax.broadcasted_iota(jnp.int32, (8, width), 0)
    pad = jnp.zeros((16, width), BF16)

    def operands(tile):
        one, two, three = split3(tile)
        mixed = jnp.where(row_id < 3, two, pltpu.roll(three, 3, 0))
        mixed = jnp.where(row_id < 6, mixed, 0.0)
        return one, two, three, jnp.concatenate([one, mixed], 0).astype(BF16)

    def prepare_near(step, carry):
        for member in range(8):
            block = 8 * step + member
            one, two, three, columns = operands(own_ref[block])
            rows = jnp.concatenate([one, one, two, two, one, three], 0).astype(BF16)
            near_turn[block] = jnp.concatenate([rows, pad], 0).T
            near_cols[block] = jnp.concatenate([columns, columns], 1)
            near_sum[block] = jnp.zeros((width, 16), F32)
        return carry

    lax.fori_loop(0, blocks // 8, prepare_near, 0)

    tile_ref[...] = jnp.zeros_like(tile_ref)

    def prepare_far(peer, carry):
        for slot in range(cap):
            tile_ref[slot, 0:3, :] = got_ref[peer, 3 * slot : 3 * slot + 3, :]
        for slot in range(cap):
            tile = tile_ref[slot]
            square = -LOG2E * jnp.sum(tile * tile, 0, keepdims=True)
            one, two, three, columns = operands(
                jnp.where(row_id == 3, square, jnp.where(row_id == 4, 1.0, scale * tile))
            )
            place = peer * cap + slot
            rows = jnp.concatenate([one, two, one, two, three, one], 0).astype(BF16)
            far_rows[place] = jnp.concatenate([rows, pad], 0)
            far_turn[place] = columns.T
            far_sum[place] = jnp.zeros((16, width), F32)
        return carry

    lax.fori_loop(0, peers, prepare_far, 0)

    def one_group(step, carry):
        results = []
        for member in range(group):
            place = step * group + member
            near, far = first_ref[place], second_ref[place]
            live = live_ref[place].astype(F32)
            power = jnp.dot(near_turn[near], far_rows[far], preferred_element_type=F32)
            weight = jnp.exp2(power)
            first = weight.astype(BF16)
            second = (weight - first.astype(F32)).astype(BF16)
            columns = far_turn[far]
            pushed = jnp.dot(
                jnp.concatenate([first, second], 1),
                jnp.concatenate([columns, columns], 0),
                preferred_element_type=F32,
            )
            recoil = jnp.dot(
                near_cols[near],
                jnp.concatenate([first, second], 0),
                preferred_element_type=F32,
            )
            results.append((near, far, live * pushed, live * recoil))
        for near, far, pushed, recoil in results:
            near_sum[near] += pushed
            far_sum[far] += recoil
        return carry

    lax.fori_loop(0, pairs // group, one_group, 0)

    def joined(sums):
        low = sums[8:16]
        return sums[:8] + jnp.where(row_id < 3, low + pltpu.roll(low, 5, 0), 0.0)

    def finish_near(step, carry):
        for member in range(8):
            block = 8 * step + member
            sums = joined(near_sum[block].T)
            seg_ref[block] = own_ref[block] * sums[4:5] - (1.0 / scale) * sums
        return carry

    lax.fori_loop(0, blocks // 8, finish_near, 0)

    def finish_far(peer, carry):
        for slot in range(cap):
            rows = slice(3 * slot, 3 * slot + 3)
            sums = joined(far_sum[peer * cap + slot])
            back_ref[peer, rows, :] = got_ref[peer, rows, :] * sums[3:4] - sums[0:3]
        back_ref[peer, 3 * cap :, :] = jnp.broadcast_to(
            ratio_ref[0:1], (back_ref.shape[1] - 3 * cap, width)
        )
        return carry

    lax.fori_loop(0, peers, finish_far, 0)


def total_kernel(
    cap,
    chunk,
    back_ref,
    send_ref,
    own_ref,
    seg_ref,
    force_ref,
    shared_ref,
    total_ref,
    lower_ref,
    upper_ref,
    step_ref,
    sums,
):
    depth = force_ref.shape[0] // 3
    blocks, width = seg_ref.shape
    sums[...] = own_ref[...]

    def give_back(peer, best):
        for slot in range(cap):
            block = send_ref[0, peer, slot]
            sums[block, 0:3, :] += back_ref[peer, 3 * slot : 3 * slot + 3, :]
        return jnp.minimum(best, back_ref[peer, 3 * cap : 3 * cap + 1, :])

    best = lax.fori_loop(
        0, back_ref.shape[0], give_back, jnp.full((1, width), jnp.inf, F32)
    )
    step_ref[...] = jnp.broadcast_to(COURANT * jnp.sqrt(best), step_ref.shape)
    total_ref[...] = force_ref[...]

    def scatter(step, carry):
        start = step * 8
        hot, mask = selectors(lane_row(seg_ref, start, 8), depth)
        rows = [
            jnp.concatenate([sums[start + block, row : row + 1, :] for block in range(8)], 1)
            for row in range(3)
        ]
        total_ref[...] += spread(rows, hot, mask)
        return carry

    lax.fori_loop(0, blocks // 8, scatter, 0)

    table = split_table(total_ref[...])

    def gather(step, carry):
        lanes = pl.ds(pl.multiple_of(step * chunk, chunk), chunk)
        for side, out_ref in ((0, upper_ref), (1, lower_ref)):
            hot, mask = selectors(shared_ref[side : side + 1, lanes], depth)
            rows = pick(table, hot, mask)
            for row in range(3):
                out_ref[row : row + 1, lanes] = rows[row]
        return carry

    lax.fori_loop(0, shared_ref.shape[1] // chunk, gather, 0)


def update_kernel(
    chunk,
    total_ref,
    lower_ref,
    upper_ref,
    shared_ref,
    mass_ref,
    vel_ref,
    disp_ref,
    step_ref,
    new_disp_ref,
    new_vel_ref,
    sums,
):
    sums[...] = total_ref[...]
    depth = sums.shape[0] // 3

    def scatter(step, carry):
        lanes = pl.ds(pl.multiple_of(step * chunk, chunk), chunk)
        for side, in_ref in ((0, lower_ref), (1, upper_ref)):
            hot, mask = selectors(shared_ref[side : side + 1, lanes], depth)
            rows = [in_ref[row : row + 1, lanes] for row in range(3)]
            sums[...] += spread(rows, hot, mask)
        return carry

    lax.fori_loop(0, shared_ref.shape[1] // chunk, scatter, 0)
    unfold(sums, new_vel_ref)
    time_step = step_ref[0:1, 0:1]
    velocity = vel_ref[...] + time_step * (new_vel_ref[...] / mass_ref[...])
    new_vel_ref[...] = velocity
    new_disp_ref[...] = disp_ref[...] + time_step * velocity


def shape(*dims):
    return jax.ShapeDtypeStruct(dims, F32)


def shards(
    ref_pos,
    displacement,
    velocity,
    node_mass,
    elem_nodes,
    elem_part,
    elem_scale,
    part_stiff,
    shared,
    seg_node,
    seg_mask,
    send_blk,
    pair_a,
    pair_slot,
    pair_mask,
):
    axes = ("grp", "dev")
    peers, cap = send_blk.shape[1:]
    nodes = node_mass.shape[0]
    blocks, width = seg_node.shape
    elems = elem_nodes.shape[1]
    pairs = pair_a.shape[0]
    share = shared.shape[1]
    depth = nodes // WIDE
    slab = -(-(3 * cap + 1) // 8) * 8
    mass = node_mass.reshape(1, -1)

    own, outgoing = pl.pallas_call(
        functools.partial(segment_kernel, cap),
        out_shape=(shape(blocks, 8, width), shape(peers, slab, width)),
        in_specs=[VMEM, VMEM, VMEM, VMEM, SMEM],
        out_specs=(VMEM, VMEM),
        scratch_shapes=[pltpu.VMEM((3 * depth, WIDE), F32), pltpu.VMEM((3, nodes), F32)],
        compiler_params=PARAMS,
        name="segments",
    )(ref_pos, displacement, seg_node, seg_mask, send_blk)
    arrived = lax.all_to_all(outgoing, axes, split_axis=0, concat_axis=0, tiled=True)

    chunk = math.gcd(elems, 512)
    work = 2 * 4 * elems * WIDE * depth
    pull, ratio = pl.pallas_call(
        functools.partial(pull_kernel, chunk),
        out_shape=(shape(12, elems), shape(8, width)),
        in_specs=[VMEM, VMEM, VMEM, VMEM, VMEM, SMEM],
        out_specs=(VMEM, VMEM),
        scratch_shapes=[pltpu.VMEM((4 * depth, WIDE), F32)],
        compiler_params=PARAMS,
        cost_estimate=pl.CostEstimate(flops=12 * work, bytes_accessed=2**20, transcendentals=0),
        name="pulls",
    )(displacement, mass, elem_nodes, elem_part.reshape(1, -1), elem_scale.reshape(1, -1), part_stiff)

    group = math.gcd(pairs, 8)
    seg_force, going_back = pl.pallas_call(
        functools.partial(pair_kernel, cap, group),
        out_shape=(shape(blocks, 8, width), shape(peers, slab, width)),
        in_specs=[VMEM, VMEM, VMEM, SMEM, SMEM, SMEM],
        out_specs=(VMEM, VMEM),
        scratch_shapes=[
            pltpu.VMEM((blocks, width, 64), BF16),
            pltpu.VMEM((blocks, 16, 2 * width), BF16),
            pltpu.VMEM((peers * cap, 64, width), BF16),
            pltpu.VMEM((peers * cap, width, 16), BF16),
            pltpu.VMEM((blocks, width, 16), F32),
            pltpu.VMEM((peers * cap, 16, width), F32),
            pltpu.VMEM((cap, 8, width), F32),
        ],
        compiler_params=PARAMS,
        name="pairs",
    )(own, arrived, ratio, pair_a, pair_slot, pair_mask)
    returned = lax.all_to_all(going_back, axes, split_axis=0, concat_axis=0, tiled=True)

    force = pl.pallas_call(
        functools.partial(force_kernel, chunk),
        out_shape=shape(3 * depth, WIDE),
        in_specs=[VMEM, VMEM, pl.BlockSpec(memory_space=pl.ANY)],
        out_specs=VMEM,
        compiler_params=PARAMS,
        cost_estimate=pl.CostEstimate(flops=12 * work, bytes_accessed=2**20, transcendentals=0),
        name="forces",
    )(pull, elem_nodes, seg_force)

    piece = math.gcd(share, 1024)
    total, lower, upper, time_step = pl.pallas_call(
        functools.partial(total_kernel, cap, piece),
        out_shape=(shape(3 * depth, WIDE), shape(3, share), shape(3, share), shape(8, width)),
        in_specs=[VMEM, SMEM, VMEM, VMEM, VMEM, VMEM],
        out_specs=(VMEM, VMEM, VMEM, VMEM),
        scratch_shapes=[pltpu.VMEM((blocks, 8, width), F32)],
        compiler_params=PARAMS,
        name="totals",
    )(returned, send_blk, seg_force, seg_node, force, shared)
    from_lower = shifted(lower, "dev", 1)
    from_upper = shifted(upper, "dev", -1)

    return pl.pallas_call(
        functools.partial(update_kernel, piece),
        out_shape=(shape(3, nodes), shape(3, nodes)),
        in_specs=[VMEM] * 8,
        out_specs=(VMEM, VMEM),
        scratch_shapes=[pltpu.VMEM((3 * depth, WIDE), F32)],
        compiler_params=PARAMS,
        name="update",
    )(total, from_lower, from_upper, shared, mass, velocity, displacement, time_step)


def solution(mesh):
    return jax.shard_map(
        shards,
        mesh=mesh,
        in_specs=(
            P(None, ("grp", "dev")),
            P(None, ("grp", "dev")),
            P(None, ("grp", "dev")),
            P(("grp", "dev")),
            P(None, ("grp", "dev")),
            P(("grp", "dev")),
            P(("grp", "dev")),
            P(("grp", "dev")),
            P(None, ("grp", "dev")),
            P(("grp", "dev"), None),
            P(("grp", "dev"), None),
            P(("grp", "dev"), None, None),
            P(("grp", "dev")),
            P(("grp", "dev")),
            P(("grp", "dev")),
        ),
        out_specs=(P(None, ("grp", "dev")), P(None, ("grp", "dev"))),
        check_vma=False,
    )
```

```python
import functools
import math

import jax
import jax.numpy as jnp
from jax import lax
from jax.experimental import pallas as pl
from jax.experimental.pallas import tpu as pltpu
from jax.sharding import PartitionSpec as P

SPRINGS = ((0, 1, 1.0), (1, 2, 1.0), (2, 3, 1.0), (3, 0, 1.0), (0, 2, 0.5), (1, 3, 0.5))
COURANT = 0.5
FAR_AWAY = 64.0
WIDE = 256
LIMIT = 56 * 1024 * 1024
F32 = jnp.float32
BF16 = jnp.bfloat16
VMEM = pl.BlockSpec(memory_space=pltpu.VMEM)
SMEM = pl.BlockSpec(memory_space=pltpu.SMEM)
PARAMS = pltpu.CompilerParams(vmem_limit_bytes=LIMIT)


def shifted(value, axis, steps):
    count = lax.axis_size(axis)
    first, last = (max(0, -steps), min(count, count - steps))
    return lax.ppermute(value, axis, [(source, source + steps) for source in range(first, last)])


def split3(x):
    first = x.astype(BF16).astype(F32)
    rest = x - first
    second = rest.astype(BF16).astype(F32)
    third = (rest - second).astype(BF16).astype(F32)
    return first, second, third


def split_table(table):
    return jnp.concatenate(split3(table), 0).astype(BF16)


def selectors(index, depth):
    count = index.shape[1]
    low = index & (WIDE - 1)
    high = index // WIDE
    hot = jnp.where(lax.broadcasted_iota(jnp.int32, (WIDE, count), 0) == low, 1.0, 0.0)
    mask = lax.broadcasted_iota(jnp.int32, (depth, count), 0) == high
    return hot.astype(BF16), mask


def pick(table, hot, mask):
    depth = mask.shape[0]
    size = table.shape[0] // 3
    parts = jnp.dot(table, hot, preferred_element_type=F32)
    whole = parts[:size] + parts[size : 2 * size] + parts[2 * size :]
    return [
        jnp.sum(jnp.where(mask, whole[row : row + depth], 0.0), 0, keepdims=True)
        for row in range(0, size, depth)
    ]


def spread(rows, hot, mask):
    firsts, seconds = [], []
    for row in rows:
        first = row.astype(BF16).astype(F32)
        firsts.append(jnp.where(mask, first, 0.0))
        seconds.append(jnp.where(mask, row - first, 0.0))
    stacked = jnp.concatenate(firsts + seconds, 0).astype(BF16)
    sums = lax.dot_general(stacked, hot, (((1,), (1,)), ((), ())), preferred_element_type=F32)
    half = sums.shape[0] // 2
    return sums[:half] + sums[half:]


def fold(ref, to_ref, first=0):
    rows, nodes = ref.shape
    depth = nodes // WIDE
    for row in range(rows):
        for high in range(depth):
            place = first + row * depth + high
            to_ref[place : place + 1, :] = ref[row : row + 1, high * WIDE : (high + 1) * WIDE]


def unfold(ref, to_ref):
    rows, nodes = to_ref.shape
    depth = nodes // WIDE
    for row in range(rows):
        for high in range(depth):
            place = row * depth + high
            to_ref[row : row + 1, high * WIDE : (high + 1) * WIDE] = ref[place : place + 1, :]


def lane_row(ref, start, count):
    tile = ref[pl.ds(pl.multiple_of(start, 8), count), :]
    return jnp.concatenate([tile[row : row + 1] for row in range(count)], 1)


def segment_kernel(
    cap, pos_ref, disp_ref, seg_ref, mask_ref, send_ref, own_ref, out_ref, table_ref, moved_ref
):
    depth = table_ref.shape[0] // 3
    blocks, width = seg_ref.shape
    moved_ref[...] = pos_ref[...] + disp_ref[...]
    fold(moved_ref, table_ref)
    table = split_table(table_ref[...])

    def gather(step, carry):
        start = step * 8
        hot, mask = selectors(lane_row(seg_ref, start, 8), depth)
        live = lane_row(mask_ref, start, 8) > 0
        rows = [jnp.where(live, row, -FAR_AWAY) for row in pick(table, hot, mask)]
        square = rows[0] * rows[0] + rows[1] * rows[1] + rows[2] * rows[2]
        rows += [jnp.ones_like(square), -square]
        for block in range(8):
            lanes = slice(block * width, (block + 1) * width)
            for row in range(5):
                own_ref[start + block, row : row + 1, :] = rows[row][:, lanes]
            own_ref[start + block, 5:8, :] = jnp.zeros((3, width), F32)
        return carry

    lax.fori_loop(0, blocks // 8, gather, 0)

    def send(peer, carry):
        for slot in range(cap):
            block = own_ref[send_ref[0, peer, slot], 0:3, :]
            out_ref[peer, 3 * slot : 3 * slot + 3, :] = jnp.where(
                block < -0.5 * FAR_AWAY, FAR_AWAY, block
            )
        out_ref[peer, 3 * cap :, :] = jnp.zeros((out_ref.shape[1] - 3 * cap, width), F32)
        return carry

    lax.fori_loop(0, out_ref.shape[0], send, 0)


def pull_kernel(
    chunk, disp_ref, mass_ref, nodes_ref, part_ref, scale_ref, stiff_ref, pull_ref, ratio_ref, table_ref
):
    depth = table_ref.shape[0] // 4
    elems = nodes_ref.shape[1]
    parts = stiff_ref.shape[0]
    fold(disp_ref, table_ref)
    fold(mass_ref, table_ref, 3 * depth)
    table = split_table(table_ref[...])

    def one_chunk(step, best):
        lanes = pl.ds(pl.multiple_of(step * chunk, chunk), chunk)
        local = lax.rem(part_ref[:, lanes], parts)
        stiff = jnp.zeros(local.shape, F32)
        for part in range(parts):
            stiff = jnp.where(local == part, stiff_ref[part], stiff)
        stiff = stiff * scale_ref[:, lanes]
        index = jnp.concatenate([nodes_ref[k : k + 1, lanes] for k in range(4)], 1)
        hot, mask = selectors(index, depth)
        rows = pick(table, hot, mask)
        corner = [[row[:, k * chunk : (k + 1) * chunk] for row in rows] for k in range(4)]
        mass = jnp.minimum(
            jnp.minimum(corner[0][3], corner[1][3]), jnp.minimum(corner[2][3], corner[3][3])
        )
        total = [[jnp.zeros_like(stiff) for axis in range(3)] for k in range(4)]
        for head, tail, weight in SPRINGS:
            for axis in range(3):
                pull = weight * stiff * (corner[tail][axis] - corner[head][axis])
                total[head][axis] = total[head][axis] + pull
                total[tail][axis] = total[tail][axis] - pull
        for axis in range(3):
            for k in range(4):
                pull_ref[4 * axis + k : 4 * axis + k + 1, lanes] = total[k][axis]
        return jnp.minimum(best, mass / stiff)

    best = lax.fori_loop(
        0, elems // chunk, one_chunk, jnp.full((1, chunk), jnp.inf, F32)
    )
    ratio_ref[...] = jnp.broadcast_to(jnp.min(best, 1, keepdims=True), ratio_ref.shape)


def force_kernel(chunk, pull_ref, nodes_ref, after_ref, force_ref):
    depth = force_ref.shape[0] // 3
    force_ref[...] = jnp.zeros_like(force_ref)

    def one_chunk(step, carry):
        lanes = pl.ds(pl.multiple_of(step * chunk, chunk), chunk)
        index = jnp.concatenate([nodes_ref[k : k + 1, lanes] for k in range(4)], 1)
        hot, mask = selectors(index, depth)
        rows = [
            jnp.concatenate([pull_ref[4 * axis + k : 4 * axis + k + 1, lanes] for k in range(4)], 1)
            for axis in range(3)
        ]
        force_ref[...] += spread(rows, hot, mask)
        return carry

    lax.fori_loop(0, nodes_ref.shape[1] // chunk, one_chunk, 0)


def pair_kernel(
    cap,
    group,
    own_ref,
    got_ref,
    ratio_ref,
    first_ref,
    second_ref,
    live_ref,
    seg_ref,
    back_ref,
    near_rows,
    near_turn,
    near_cols,
    far_rows,
    far_turn,
    far_cols,
    near_sum,
    far_sum,
    tile_ref,
):
    blocks, _, width = own_ref.shape
    peers = got_ref.shape[0]
    pairs = first_ref.shape[0]
    scale = 2.0

    row_id = lax.broadcasted_iota(jnp.int32, (8, width), 0)
    pad = jnp.zeros((16, width), BF16)
    gap = jnp.zeros((64, width), BF16)

    def operands(tile):
        one, two, three = split3(tile)
        mixed = jnp.where(row_id < 3, two, pltpu.roll(three, 3, 0))
        mixed = jnp.where(row_id < 6, mixed, 0.0)
        columns = jnp.concatenate([one, mixed], 0)
        return one, two, three, jnp.concatenate([columns, columns], 1).astype(BF16)

    def prepare_near(step, carry):
        for member in range(8):
            block = 8 * step + member
            one, two, three, columns = operands(own_ref[block])
            rows = jnp.concatenate([one, one, two, two, one, three], 0).astype(BF16)
            rows = jnp.concatenate([rows, pad], 0)
            near_rows[block] = rows
            near_turn[block] = jnp.concatenate([rows, gap], 0).T
            near_cols[block] = columns
            near_sum[block] = jnp.zeros((16, width), F32)
        return carry

    lax.fori_loop(0, blocks // 8, prepare_near, 0)

    tile_ref[...] = jnp.zeros_like(tile_ref)

    several = math.gcd(peers, 4)

    def prepare_far(step, carry):
        places = [(several * step + k, slot) for k in range(several) for slot in range(cap)]
        for member, (peer, slot) in enumerate(places):
            tile_ref[member, 0:3, :] = got_ref[peer, 3 * slot : 3 * slot + 3, :]
        for member, (peer, slot) in enumerate(places):
            tile = tile_ref[member]
            square = -jnp.sum(tile * tile, 0, keepdims=True)
            one, two, three, columns = operands(
                jnp.where(row_id == 3, square, jnp.where(row_id == 4, 1.0, scale * tile))
            )
            place = peer * cap + slot
            rows = jnp.concatenate([one, two, one, two, three, one], 0).astype(BF16)
            rows = jnp.concatenate([rows, pad], 0)
            far_rows[place] = rows
            far_turn[place] = jnp.concatenate([gap, rows], 0).T
            far_cols[place] = columns
            far_sum[place] = jnp.zeros((16, width), F32)
        return carry

    lax.fori_loop(0, peers // several, prepare_far, 0)

    def one_group(step, carry):
        results = []
        for member in range(group):
            place = step * group + member
            near, far = first_ref[place], second_ref[place]
            live = live_ref[place].astype(F32)
            right = jnp.concatenate(
                [
                    jnp.concatenate([far_rows[far], gap], 1),
                    jnp.concatenate([gap, near_rows[near]], 1),
                ],
                0,
            )
            both = jnp.dot(
                near_turn[near] + far_turn[far], right, preferred_element_type=F32
            )
            weight = jnp.exp(both)
            first = weight.astype(BF16)
            second = (weight - first.astype(F32)).astype(BF16)
            sums = jnp.dot(
                jnp.concatenate([near_cols[near], far_cols[far]], 0),
                jnp.concatenate([first, second], 0),
                preferred_element_type=F32,
            )
            results.append((near, far, live * sums[16:, width:], live * sums[:16, :width]))
        for near, far, pushed, recoil in results:
            near_sum[near] += pushed
            far_sum[far] += recoil
        return carry

    lax.fori_loop(0, pairs // group, one_group, 0)

    def joined(sums):
        low = sums[8:16]
        return sums[:8] + jnp.where(row_id < 3, low + pltpu.roll(low, 5, 0), 0.0)

    def finish_near(step, carry):
        for member in range(8):
            block = 8 * step + member
            sums = joined(near_sum[block])
            seg_ref[block] = own_ref[block] * sums[4:5] - (1.0 / scale) * sums
        return carry

    lax.fori_loop(0, blocks // 8, finish_near, 0)

    def finish_far(step, carry):
        for peer in [several * step + k for k in range(several)]:
            for slot in range(cap):
                rows = slice(3 * slot, 3 * slot + 3)
                sums = joined(far_sum[peer * cap + slot])
                back_ref[peer, rows, :] = got_ref[peer, rows, :] * sums[3:4] - sums[0:3]
            back_ref[peer, 3 * cap :, :] = jnp.broadcast_to(
                ratio_ref[0:1], (back_ref.shape[1] - 3 * cap, width)
            )
        return carry

    lax.fori_loop(0, peers // several, finish_far, 0)


def total_kernel(
    cap,
    chunk,
    back_ref,
    send_ref,
    own_ref,
    seg_ref,
    force_ref,
    shared_ref,
    total_ref,
    lower_ref,
    upper_ref,
    step_ref,
    sums,
):
    depth = force_ref.shape[0] // 3
    blocks, width = seg_ref.shape
    sums[...] = own_ref[...]

    def give_back(peer, best):
        for slot in range(cap):
            block = send_ref[0, peer, slot]
            sums[block, 0:3, :] += back_ref[peer, 3 * slot : 3 * slot + 3, :]
        return jnp.minimum(best, back_ref[peer, 3 * cap : 3 * cap + 1, :])

    best = lax.fori_loop(
        0, back_ref.shape[0], give_back, jnp.full((1, width), jnp.inf, F32)
    )
    step_ref[...] = jnp.broadcast_to(COURANT * jnp.sqrt(best), step_ref.shape)
    total_ref[...] = force_ref[...]

    def scatter(step, carry):
        start = step * 8
        hot, mask = selectors(lane_row(seg_ref, start, 8), depth)
        rows = [
            jnp.concatenate([sums[start + block, row : row + 1, :] for block in range(8)], 1)
            for row in range(3)
        ]
        total_ref[...] += spread(rows, hot, mask)
        return carry

    lax.fori_loop(0, blocks // 8, scatter, 0)

    table = split_table(total_ref[...])

    def gather(step, carry):
        lanes = pl.ds(pl.multiple_of(step * chunk, chunk), chunk)
        for side, out_ref in ((0, upper_ref), (1, lower_ref)):
            hot, mask = selectors(shared_ref[side : side + 1, lanes], depth)
            rows = pick(table, hot, mask)
            for row in range(3):
                out_ref[row : row + 1, lanes] = rows[row]
        return carry

    lax.fori_loop(0, shared_ref.shape[1] // chunk, gather, 0)


def update_kernel(
    chunk,
    total_ref,
    lower_ref,
    upper_ref,
    shared_ref,
    mass_ref,
    vel_ref,
    disp_ref,
    step_ref,
    new_disp_ref,
    new_vel_ref,
    sums,
):
    sums[...] = total_ref[...]
    depth = sums.shape[0] // 3

    def scatter(step, carry):
        lanes = pl.ds(pl.multiple_of(step * chunk, chunk), chunk)
        for side, in_ref in ((0, lower_ref), (1, upper_ref)):
            hot, mask = selectors(shared_ref[side : side + 1, lanes], depth)
            rows = [in_ref[row : row + 1, lanes] for row in range(3)]
            sums[...] += spread(rows, hot, mask)
        return carry

    lax.fori_loop(0, shared_ref.shape[1] // chunk, scatter, 0)
    unfold(sums, new_vel_ref)
    time_step = step_ref[0:1, 0:1]
    velocity = vel_ref[...] + time_step * (new_vel_ref[...] / mass_ref[...])
    new_vel_ref[...] = velocity
    new_disp_ref[...] = disp_ref[...] + time_step * velocity


def shape(*dims):
    return jax.ShapeDtypeStruct(dims, F32)


def shards(
    ref_pos,
    displacement,
    velocity,
    node_mass,
    elem_nodes,
    elem_part,
    elem_scale,
    part_stiff,
    shared,
    seg_node,
    seg_mask,
    send_blk,
    pair_a,
    pair_slot,
    pair_mask,
):
    axes = ("grp", "dev")
    peers, cap = send_blk.shape[1:]
    nodes = node_mass.shape[0]
    blocks, width = seg_node.shape
    elems = elem_nodes.shape[1]
    pairs = pair_a.shape[0]
    share = shared.shape[1]
    depth = nodes // WIDE
    slab = -(-(3 * cap + 1) // 8) * 8
    mass = node_mass.reshape(1, -1)

    own, outgoing = pl.pallas_call(
        functools.partial(segment_kernel, cap),
        out_shape=(shape(blocks, 8, width), shape(peers, slab, width)),
        in_specs=[VMEM, VMEM, VMEM, VMEM, SMEM],
        out_specs=(VMEM, VMEM),
        scratch_shapes=[pltpu.VMEM((3 * depth, WIDE), F32), pltpu.VMEM((3, nodes), F32)],
        compiler_params=PARAMS,
        name="segments",
    )(ref_pos, displacement, seg_node, seg_mask, send_blk)
    arrived = lax.all_to_all(outgoing, axes, split_axis=0, concat_axis=0, tiled=True)

    chunk = math.gcd(elems, 1024)
    work = 2 * 4 * elems * WIDE * depth
    pull, ratio = pl.pallas_call(
        functools.partial(pull_kernel, chunk),
        out_shape=(shape(12, elems), shape(8, width)),
        in_specs=[VMEM, VMEM, VMEM, VMEM, VMEM, SMEM],
        out_specs=(VMEM, VMEM),
        scratch_shapes=[pltpu.VMEM((4 * depth, WIDE), F32)],
        compiler_params=PARAMS,
        cost_estimate=pl.CostEstimate(flops=12 * work, bytes_accessed=2**20, transcendentals=0),
        name="pulls",
    )(displacement, mass, elem_nodes, elem_part.reshape(1, -1), elem_scale.reshape(1, -1), part_stiff)

    group = math.gcd(pairs, 32)
    seg_force, going_back = pl.pallas_call(
        functools.partial(pair_kernel, cap, group),
        out_shape=(shape(blocks, 8, width), shape(peers, slab, width)),
        in_specs=[VMEM, VMEM, VMEM, SMEM, SMEM, SMEM],
        out_specs=(VMEM, VMEM),
        scratch_shapes=[
            pltpu.VMEM((blocks, 64, width), BF16),
            pltpu.VMEM((blocks, width, width), BF16),
            pltpu.VMEM((blocks, 16, 2 * width), BF16),
            pltpu.VMEM((peers * cap, 64, width), BF16),
            pltpu.VMEM((peers * cap, width, width), BF16),
            pltpu.VMEM((peers * cap, 16, 2 * width), BF16),
            pltpu.VMEM((blocks, 16, width), F32),
            pltpu.VMEM((peers * cap, 16, width), F32),
            pltpu.VMEM((4 * cap, 8, width), F32),
        ],
        compiler_params=PARAMS,
        name="pairs",
    )(own, arrived, ratio, pair_a, pair_slot, pair_mask)
    returned = lax.all_to_all(going_back, axes, split_axis=0, concat_axis=0, tiled=True)

    force = pl.pallas_call(
        functools.partial(force_kernel, chunk),
        out_shape=shape(3 * depth, WIDE),
        in_specs=[VMEM, VMEM, pl.BlockSpec(memory_space=pl.ANY)],
        out_specs=VMEM,
        compiler_params=PARAMS,
        cost_estimate=pl.CostEstimate(flops=12 * work, bytes_accessed=2**20, transcendentals=0),
        name="forces",
    )(pull, elem_nodes, seg_force)

    piece = math.gcd(share, 1024)
    total, lower, upper, time_step = pl.pallas_call(
        functools.partial(total_kernel, cap, piece),
        out_shape=(shape(3 * depth, WIDE), shape(3, share), shape(3, share), shape(8, width)),
        in_specs=[VMEM, SMEM, VMEM, VMEM, VMEM, VMEM],
        out_specs=(VMEM, VMEM, VMEM, VMEM),
        scratch_shapes=[pltpu.VMEM((blocks, 8, width), F32)],
        compiler_params=PARAMS,
        name="totals",
    )(returned, send_blk, seg_force, seg_node, force, shared)
    from_lower = shifted(lower, "dev", 1)
    from_upper = shifted(upper, "dev", -1)

    return pl.pallas_call(
        functools.partial(update_kernel, piece),
        out_shape=(shape(3, nodes), shape(3, nodes)),
        in_specs=[VMEM] * 8,
        out_specs=(VMEM, VMEM),
        scratch_shapes=[pltpu.VMEM((3 * depth, WIDE), F32)],
        compiler_params=PARAMS,
        name="update",
    )(total, from_lower, from_upper, shared, mass, velocity, displacement, time_step)


def solution(mesh):
    return jax.shard_map(
        shards,
        mesh=mesh,
        in_specs=(
            P(None, ("grp", "dev")),
            P(None, ("grp", "dev")),
            P(None, ("grp", "dev")),
            P(("grp", "dev")),
            P(None, ("grp", "dev")),
            P(("grp", "dev")),
            P(("grp", "dev")),
            P(("grp", "dev")),
            P(None, ("grp", "dev")),
            P(("grp", "dev"), None),
            P(("grp", "dev"), None),
            P(("grp", "dev"), None, None),
            P(("grp", "dev")),
            P(("grp", "dev")),
            P(("grp", "dev")),
        ),
        out_specs=(P(None, ("grp", "dev")), P(None, ("grp", "dev"))),
        check_vma=False,
    )
```

```python
import functools
import math

import jax
import jax.numpy as jnp
from jax import lax
from jax.experimental import pallas as pl
from jax.experimental.pallas import tpu as pltpu
from jax.sharding import PartitionSpec as P

SPRINGS = ((0, 1, 1.0), (1, 2, 1.0), (2, 3, 1.0), (3, 0, 1.0), (0, 2, 0.5), (1, 3, 0.5))
COURANT = 0.5
FAR_AWAY = 64.0
WIDE = 256
LIMIT = 56 * 1024 * 1024
F32 = jnp.float32
BF16 = jnp.bfloat16
VMEM = pl.BlockSpec(memory_space=pltpu.VMEM)
SMEM = pl.BlockSpec(memory_space=pltpu.SMEM)
PARAMS = pltpu.CompilerParams(vmem_limit_bytes=LIMIT)


def split3(x):
    first = x.astype(BF16).astype(F32)
    rest = x - first
    second = rest.astype(BF16).astype(F32)
    third = (rest - second).astype(BF16).astype(F32)
    return first, second, third


def split_table(table):
    return jnp.concatenate(split3(table), 0).astype(BF16)


def selectors(index, depth):
    count = index.shape[1]
    low = index & (WIDE - 1)
    high = index // WIDE
    hot = jnp.where(lax.broadcasted_iota(jnp.int32, (WIDE, count), 0) == low, 1.0, 0.0)
    mask = lax.broadcasted_iota(jnp.int32, (depth, count), 0) == high
    return hot.astype(BF16), mask


def pick(table, hot, mask):
    depth = mask.shape[0]
    size = table.shape[0] // 3
    parts = jnp.dot(table, hot, preferred_element_type=F32)
    whole = parts[:size] + parts[size : 2 * size] + parts[2 * size :]
    return [
        jnp.sum(jnp.where(mask, whole[row : row + depth], 0.0), 0, keepdims=True)
        for row in range(0, size, depth)
    ]


def spread(rows, hot, mask):
    firsts, seconds = [], []
    for row in rows:
        first = row.astype(BF16).astype(F32)
        firsts.append(jnp.where(mask, first, 0.0))
        seconds.append(jnp.where(mask, row - first, 0.0))
    stacked = jnp.concatenate(firsts + seconds, 0).astype(BF16)
    sums = lax.dot_general(stacked, hot, (((1,), (1,)), ((), ())), preferred_element_type=F32)
    half = sums.shape[0] // 2
    return sums[:half] + sums[half:]


def fold(ref, to_ref, first=0):
    rows, nodes = ref.shape
    depth = nodes // WIDE
    for row in range(rows):
        for high in range(depth):
            place = first + row * depth + high
            to_ref[place : place + 1, :] = ref[row : row + 1, high * WIDE : (high + 1) * WIDE]


def unfold(ref, to_ref):
    rows, nodes = to_ref.shape
    depth = nodes // WIDE
    for row in range(rows):
        for high in range(depth):
            place = row * depth + high
            to_ref[row : row + 1, high * WIDE : (high + 1) * WIDE] = ref[place : place + 1, :]


def lane_row(ref, start, count):
    tile = ref[pl.ds(pl.multiple_of(start, 8), count), :]
    return jnp.concatenate([tile[row : row + 1] for row in range(count)], 1)


def segment_kernel(
    cap, pos_ref, disp_ref, seg_ref, mask_ref, send_ref, own_ref, out_ref, table_ref, moved_ref
):
    depth = table_ref.shape[0] // 3
    blocks, width = seg_ref.shape
    moved_ref[...] = pos_ref[...] + disp_ref[...]
    fold(moved_ref, table_ref)
    table = split_table(table_ref[...])

    many = math.gcd(blocks, 16)

    def gather(step, carry):
        start = step * many
        hot, mask = selectors(lane_row(seg_ref, start, many), depth)
        live = lane_row(mask_ref, start, many) > 0
        rows = [jnp.where(live, row, -FAR_AWAY) for row in pick(table, hot, mask)]
        square = rows[0] * rows[0] + rows[1] * rows[1] + rows[2] * rows[2]
        rows += [jnp.ones_like(square), -square]
        for block in range(many):
            lanes = slice(block * width, (block + 1) * width)
            for row in range(5):
                own_ref[start + block, row : row + 1, :] = rows[row][:, lanes]
            own_ref[start + block, 5:8, :] = jnp.zeros((3, width), F32)
        return carry

    lax.fori_loop(0, blocks // many, gather, 0)

    several = math.gcd(out_ref.shape[0], 8)

    def send(step, carry):
        for peer in [several * step + k for k in range(several)]:
            for slot in range(cap):
                block = own_ref[send_ref[peer * cap + slot], 0:3, :]
                out_ref[peer, 3 * slot : 3 * slot + 3, :] = jnp.where(
                    block < -0.5 * FAR_AWAY, FAR_AWAY, block
                )
            out_ref[peer, 3 * cap :, :] = jnp.zeros((out_ref.shape[1] - 3 * cap, width), F32)
        return carry

    lax.fori_loop(0, out_ref.shape[0] // several, send, 0)


def pull_kernel(
    chunk, disp_ref, mass_ref, nodes_ref, part_ref, scale_ref, stiff_ref, pull_ref, ratio_ref, table_ref
):
    depth = table_ref.shape[0] // 4
    elems = nodes_ref.shape[1]
    parts = stiff_ref.shape[0]
    fold(disp_ref, table_ref)
    fold(mass_ref, table_ref, 3 * depth)
    table = split_table(table_ref[...])

    def one_chunk(step, best):
        lanes = pl.ds(pl.multiple_of(step * chunk, chunk), chunk)
        local = lax.rem(part_ref[:, lanes], parts)
        stiff = jnp.zeros(local.shape, F32)
        for part in range(parts):
            stiff = jnp.where(local == part, stiff_ref[part], stiff)
        stiff = stiff * scale_ref[:, lanes]
        index = jnp.concatenate([nodes_ref[k : k + 1, lanes] for k in range(4)], 1)
        hot, mask = selectors(index, depth)
        rows = pick(table, hot, mask)
        corner = [[row[:, k * chunk : (k + 1) * chunk] for row in rows] for k in range(4)]
        mass = jnp.minimum(
            jnp.minimum(corner[0][3], corner[1][3]), jnp.minimum(corner[2][3], corner[3][3])
        )
        total = [[jnp.zeros_like(stiff) for axis in range(3)] for k in range(4)]
        for head, tail, weight in SPRINGS:
            for axis in range(3):
                pull = weight * stiff * (corner[tail][axis] - corner[head][axis])
                total[head][axis] = total[head][axis] + pull
                total[tail][axis] = total[tail][axis] - pull
        for axis in range(3):
            for k in range(4):
                pull_ref[4 * axis + k : 4 * axis + k + 1, lanes] = total[k][axis]
        return jnp.minimum(best, mass / stiff)

    best = lax.fori_loop(
        0, elems // chunk, one_chunk, jnp.full((1, chunk), jnp.inf, F32)
    )
    ratio_ref[...] = jnp.broadcast_to(jnp.min(best, 1, keepdims=True), ratio_ref.shape)


def force_kernel(chunk, pull_ref, nodes_ref, after_ref, force_ref):
    depth = force_ref.shape[0] // 3
    force_ref[...] = jnp.zeros_like(force_ref)

    def one_chunk(step, carry):
        lanes = pl.ds(pl.multiple_of(step * chunk, chunk), chunk)
        index = jnp.concatenate([nodes_ref[k : k + 1, lanes] for k in range(4)], 1)
        hot, mask = selectors(index, depth)
        rows = [
            jnp.concatenate([pull_ref[4 * axis + k : 4 * axis + k + 1, lanes] for k in range(4)], 1)
            for axis in range(3)
        ]
        force_ref[...] += spread(rows, hot, mask)
        return carry

    lax.fori_loop(0, nodes_ref.shape[1] // chunk, one_chunk, 0)


def pair_kernel(
    cap,
    group,
    own_ref,
    got_ref,
    ratio_ref,
    first_ref,
    second_ref,
    live_ref,
    seg_ref,
    back_ref,
    near_rows,
    near_turn,
    near_cols,
    far_rows,
    far_turn,
    far_cols,
    near_sum,
    far_sum,
    tile_ref,
):
    blocks, _, width = own_ref.shape
    peers = got_ref.shape[0]
    pairs = first_ref.shape[0]
    scale = 2.0

    row_id = lax.broadcasted_iota(jnp.int32, (8, width), 0)
    pad = jnp.zeros((16, width), BF16)
    gap = jnp.zeros((64, width), BF16)

    def operands(tile):
        one, two, three = split3(tile)
        mixed = jnp.where(row_id < 3, two, pltpu.roll(three, 3, 0))
        mixed = jnp.where(row_id < 6, mixed, 0.0)
        columns = jnp.concatenate([one, mixed], 0)
        return one, two, three, jnp.concatenate([columns, columns], 1).astype(BF16)

    def prepare_near(step, carry):
        for member in range(8):
            block = 8 * step + member
            one, two, three, columns = operands(own_ref[block])
            rows = jnp.concatenate([one, one, two, two, one, three], 0).astype(BF16)
            rows = jnp.concatenate([rows, pad], 0)
            near_rows[block] = rows
            near_turn[block] = jnp.concatenate([rows, gap], 0).T
            near_cols[block] = columns
            near_sum[block] = jnp.zeros((16, width), F32)
        return carry

    lax.fori_loop(0, blocks // 8, prepare_near, 0)

    tile_ref[...] = jnp.zeros_like(tile_ref)

    several = math.gcd(peers, 4)

    def prepare_far(step, carry):
        places = [(several * step + k, slot) for k in range(several) for slot in range(cap)]
        for member, (peer, slot) in enumerate(places):
            tile_ref[member, 0:3, :] = got_ref[peer, 3 * slot : 3 * slot + 3, :]
        for member, (peer, slot) in enumerate(places):
            tile = tile_ref[member]
            square = -jnp.sum(tile * tile, 0, keepdims=True)
            one, two, three, columns = operands(
                jnp.where(row_id == 3, square, jnp.where(row_id == 4, 1.0, scale * tile))
            )
            place = peer * cap + slot
            rows = jnp.concatenate([one, two, one, two, three, one], 0).astype(BF16)
            rows = jnp.concatenate([rows, pad], 0)
            far_rows[place] = rows
            far_turn[place] = jnp.concatenate([gap, rows], 0).T
            far_cols[place] = columns
            far_sum[place] = jnp.zeros((16, width), F32)
        return carry

    lax.fori_loop(0, peers // several, prepare_far, 0)

    def one_group(step, carry):
        results = []
        for member in range(group):
            place = step * group + member
            near, far = first_ref[place], second_ref[place]
            live = live_ref[place].astype(F32)
            right = jnp.concatenate(
                [
                    jnp.concatenate([far_rows[far], gap], 1),
                    jnp.concatenate([gap, near_rows[near]], 1),
                ],
                0,
            )
            both = jnp.dot(
                near_turn[near] + far_turn[far], right, preferred_element_type=F32
            )
            weight = jnp.exp(both)
            first = weight.astype(BF16)
            second = (weight - first.astype(F32)).astype(BF16)
            sums = jnp.dot(
                jnp.concatenate([near_cols[near], far_cols[far]], 0),
                jnp.concatenate([first, second], 0),
                preferred_element_type=F32,
            )
            results.append((near, far, live * sums[16:, width:], live * sums[:16, :width]))
        for near, far, pushed, recoil in results:
            near_sum[near] += pushed
            far_sum[far] += recoil
        return carry

    lax.fori_loop(0, pairs // group, one_group, 0)

    def joined(sums):
        low = sums[8:16]
        return sums[:8] + jnp.where(row_id < 3, low + pltpu.roll(low, 5, 0), 0.0)

    def finish_near(step, carry):
        for member in range(8):
            block = 8 * step + member
            sums = joined(near_sum[block])
            seg_ref[block] = own_ref[block] * sums[4:5] - (1.0 / scale) * sums
        return carry

    lax.fori_loop(0, blocks // 8, finish_near, 0)

    def finish_far(step, carry):
        for peer in [several * step + k for k in range(several)]:
            for slot in range(cap):
                rows = slice(3 * slot, 3 * slot + 3)
                sums = joined(far_sum[peer * cap + slot])
                back_ref[peer, rows, :] = got_ref[peer, rows, :] * sums[3:4] - sums[0:3]
            back_ref[peer, 3 * cap :, :] = jnp.broadcast_to(
                ratio_ref[0:1], (back_ref.shape[1] - 3 * cap, width)
            )
        return carry

    lax.fori_loop(0, peers // several, finish_far, 0)


def total_kernel(
    cap,
    chunk,
    back_ref,
    send_ref,
    own_ref,
    seg_ref,
    force_ref,
    shared_ref,
    total_ref,
    lower_ref,
    upper_ref,
    step_ref,
    sums,
):
    depth = force_ref.shape[0] // 3
    blocks, width = seg_ref.shape
    sums[...] = own_ref[...]

    peers = back_ref.shape[0]
    several = math.gcd(peers, 8)

    def give_back(step, best):
        for peer in [several * step + k for k in range(several)]:
            for slot in range(cap):
                block = send_ref[peer * cap + slot]
                sums[block, 0:3, :] += back_ref[peer, 3 * slot : 3 * slot + 3, :]
            best = jnp.minimum(best, back_ref[peer, 3 * cap : 3 * cap + 1, :])
        return best

    best = lax.fori_loop(
        0, peers // several, give_back, jnp.full((1, width), jnp.inf, F32)
    )
    step_ref[...] = jnp.broadcast_to(COURANT * jnp.sqrt(best), step_ref.shape)
    total_ref[...] = force_ref[...]

    many = math.gcd(blocks, 16)

    def scatter(step, carry):
        start = step * many
        hot, mask = selectors(lane_row(seg_ref, start, many), depth)
        rows = [
            jnp.concatenate([sums[start + block, row : row + 1, :] for block in range(many)], 1)
            for row in range(3)
        ]
        total_ref[...] += spread(rows, hot, mask)
        return carry

    lax.fori_loop(0, blocks // many, scatter, 0)

    table = split_table(total_ref[...])

    def gather(step, carry):
        lanes = pl.ds(pl.multiple_of(step * chunk, chunk), chunk)
        index = jnp.concatenate([shared_ref[side : side + 1, lanes] for side in range(2)], 1)
        rows = pick(table, *selectors(index, depth))
        for row in range(3):
            upper_ref[row : row + 1, lanes] = rows[row][:, :chunk]
            lower_ref[row : row + 1, lanes] = rows[row][:, chunk:]
        return carry

    lax.fori_loop(0, shared_ref.shape[1] // chunk, gather, 0)


def update_kernel(
    chunk,
    total_ref,
    lower_ref,
    upper_ref,
    shared_ref,
    mass_ref,
    vel_ref,
    disp_ref,
    step_ref,
    new_disp_ref,
    new_vel_ref,
    sums,
    got_lower,
    got_upper,
    sent,
    received,
):
    me = lax.axis_index("dev")
    last = lax.axis_size("dev") - 1
    prev = {"dev": jnp.maximum(me - 1, 0)}
    following = {"dev": jnp.minimum(me + 1, last)}
    upward = pltpu.make_async_remote_copy(
        src_ref=lower_ref,
        dst_ref=got_lower,
        send_sem=sent.at[0],
        recv_sem=received.at[0],
        device_id=following,
        device_id_type=pl.DeviceIdType.MESH,
    )
    downward = pltpu.make_async_remote_copy(
        src_ref=upper_ref,
        dst_ref=got_upper,
        send_sem=sent.at[1],
        recv_sem=received.at[1],
        device_id=prev,
        device_id_type=pl.DeviceIdType.MESH,
    )
    barrier = pltpu.get_barrier_semaphore()

    @pl.when(me > 0)
    def _():
        pl.semaphore_signal(barrier, 1, device_id=prev, device_id_type=pl.DeviceIdType.MESH)

    @pl.when(me < last)
    def _():
        pl.semaphore_signal(barrier, 1, device_id=following, device_id_type=pl.DeviceIdType.MESH)

    pl.semaphore_wait(barrier, jnp.minimum(me, 1) + jnp.minimum(last - me, 1))

    @pl.when(me < last)
    def _():
        upward.start()

    @pl.when(me > 0)
    def _():
        downward.start()

    sums[...] = total_ref[...]
    depth = sums.shape[0] // 3

    @pl.when(me == 0)
    def _():
        got_lower[...] = jnp.zeros_like(got_lower)

    @pl.when(me == last)
    def _():
        got_upper[...] = jnp.zeros_like(got_upper)

    @pl.when(me > 0)
    def _():
        upward.wait_recv()

    @pl.when(me < last)
    def _():
        downward.wait_recv()

    def scatter(step, carry):
        lanes = pl.ds(pl.multiple_of(step * chunk, chunk), chunk)
        index = jnp.concatenate([shared_ref[side : side + 1, lanes] for side in range(2)], 1)
        rows = [
            jnp.concatenate([got_lower[row : row + 1, lanes], got_upper[row : row + 1, lanes]], 1)
            for row in range(3)
        ]
        sums[...] += spread(rows, *selectors(index, depth))
        return carry

    lax.fori_loop(0, shared_ref.shape[1] // chunk, scatter, 0)
    unfold(sums, new_vel_ref)
    time_step = step_ref[0:1, 0:1]
    velocity = vel_ref[...] + time_step * (new_vel_ref[...] / mass_ref[...])
    new_vel_ref[...] = velocity
    new_disp_ref[...] = disp_ref[...] + time_step * velocity

    @pl.when(me < last)
    def _():
        upward.wait_send()

    @pl.when(me > 0)
    def _():
        downward.wait_send()


def shape(*dims):
    return jax.ShapeDtypeStruct(dims, F32)


def shards(
    ref_pos,
    displacement,
    velocity,
    node_mass,
    elem_nodes,
    elem_part,
    elem_scale,
    part_stiff,
    shared,
    seg_node,
    seg_mask,
    send_blk,
    pair_a,
    pair_slot,
    pair_mask,
):
    axes = ("grp", "dev")
    peers, cap = send_blk.shape[1:]
    nodes = node_mass.shape[0]
    blocks, width = seg_node.shape
    elems = elem_nodes.shape[1]
    pairs = pair_a.shape[0]
    share = shared.shape[1]
    depth = nodes // WIDE
    slab = -(-(3 * cap + 1) // 8) * 8
    mass = node_mass.reshape(1, -1)
    send = send_blk.reshape(-1)

    own, outgoing = pl.pallas_call(
        functools.partial(segment_kernel, cap),
        out_shape=(shape(blocks, 8, width), shape(peers, slab, width)),
        in_specs=[VMEM, VMEM, VMEM, VMEM, SMEM],
        out_specs=(VMEM, VMEM),
        scratch_shapes=[pltpu.VMEM((3 * depth, WIDE), F32), pltpu.VMEM((3, nodes), F32)],
        compiler_params=PARAMS,
        name="segments",
    )(ref_pos, displacement, seg_node, seg_mask, send)
    arrived = lax.all_to_all(outgoing, axes, split_axis=0, concat_axis=0, tiled=True)

    chunk = math.gcd(elems, 1024)
    work = 2 * 4 * elems * WIDE * depth
    pull, ratio = pl.pallas_call(
        functools.partial(pull_kernel, chunk),
        out_shape=(shape(12, elems), shape(8, width)),
        in_specs=[VMEM, VMEM, VMEM, VMEM, VMEM, SMEM],
        out_specs=(VMEM, VMEM),
        scratch_shapes=[pltpu.VMEM((4 * depth, WIDE), F32)],
        compiler_params=PARAMS,
        cost_estimate=pl.CostEstimate(flops=12 * work, bytes_accessed=2**20, transcendentals=0),
        name="pulls",
    )(displacement, mass, elem_nodes, elem_part.reshape(1, -1), elem_scale.reshape(1, -1), part_stiff)

    group = math.gcd(pairs, 64)
    seg_force, going_back = pl.pallas_call(
        functools.partial(pair_kernel, cap, group),
        out_shape=(shape(blocks, 8, width), shape(peers, slab, width)),
        in_specs=[VMEM, VMEM, VMEM, SMEM, SMEM, SMEM],
        out_specs=(VMEM, VMEM),
        scratch_shapes=[
            pltpu.VMEM((blocks, 64, width), BF16),
            pltpu.VMEM((blocks, width, width), BF16),
            pltpu.VMEM((blocks, 16, 2 * width), BF16),
            pltpu.VMEM((peers * cap, 64, width), BF16),
            pltpu.VMEM((peers * cap, width, width), BF16),
            pltpu.VMEM((peers * cap, 16, 2 * width), BF16),
            pltpu.VMEM((blocks, 16, width), F32),
            pltpu.VMEM((peers * cap, 16, width), F32),
            pltpu.VMEM((4 * cap, 8, width), F32),
        ],
        compiler_params=PARAMS,
        name="pairs",
    )(own, arrived, ratio, pair_a, pair_slot, pair_mask)
    returned = lax.all_to_all(going_back, axes, split_axis=0, concat_axis=0, tiled=True)

    force = pl.pallas_call(
        functools.partial(force_kernel, chunk),
        out_shape=shape(3 * depth, WIDE),
        in_specs=[VMEM, VMEM, pl.BlockSpec(memory_space=pl.ANY)],
        out_specs=VMEM,
        compiler_params=PARAMS,
        cost_estimate=pl.CostEstimate(flops=12 * work, bytes_accessed=2**20, transcendentals=0),
        name="forces",
    )(pull, elem_nodes, seg_force)

    piece = math.gcd(share, 2048)
    total, lower, upper, time_step = pl.pallas_call(
        functools.partial(total_kernel, cap, piece),
        out_shape=(shape(3 * depth, WIDE), shape(3, share), shape(3, share), shape(8, width)),
        in_specs=[VMEM, SMEM, VMEM, VMEM, VMEM, VMEM],
        out_specs=(VMEM, VMEM, VMEM, VMEM),
        scratch_shapes=[pltpu.VMEM((blocks, 8, width), F32)],
        compiler_params=PARAMS,
        name="totals",
    )(returned, send, seg_force, seg_node, force, shared)

    return pl.pallas_call(
        functools.partial(update_kernel, piece),
        out_shape=(shape(3, nodes), shape(3, nodes)),
        in_specs=[VMEM] * 8,
        out_specs=(VMEM, VMEM),
        scratch_shapes=[
            pltpu.VMEM((3 * depth, WIDE), F32),
            pltpu.VMEM((3, share), F32),
            pltpu.VMEM((3, share), F32),
            pltpu.SemaphoreType.DMA((2,)),
            pltpu.SemaphoreType.DMA((2,)),
        ],
        compiler_params=pltpu.CompilerParams(
            vmem_limit_bytes=LIMIT, collective_id=0, has_side_effects=True
        ),
        name="update",
    )(total, lower, upper, shared, mass, velocity, displacement, time_step)


def solution(mesh):
    return jax.shard_map(
        shards,
        mesh=mesh,
        in_specs=(
            P(None, ("grp", "dev")),
            P(None, ("grp", "dev")),
            P(None, ("grp", "dev")),
            P(("grp", "dev")),
            P(None, ("grp", "dev")),
            P(("grp", "dev")),
            P(("grp", "dev")),
            P(("grp", "dev")),
            P(None, ("grp", "dev")),
            P(("grp", "dev"), None),
            P(("grp", "dev"), None),
            P(("grp", "dev"), None, None),
            P(("grp", "dev")),
            P(("grp", "dev")),
            P(("grp", "dev")),
        ),
        out_specs=(P(None, ("grp", "dev")), P(None, ("grp", "dev"))),
        check_vma=False,
    )
```

```python
import functools
import math

import jax
import jax.numpy as jnp
from jax import lax
from jax.experimental import pallas as pl
from jax.experimental.pallas import tpu as pltpu
from jax.sharding import PartitionSpec as P

SPRINGS = ((0, 1, 1.0), (1, 2, 1.0), (2, 3, 1.0), (3, 0, 1.0), (0, 2, 0.5), (1, 3, 0.5))
COURANT = 0.5
FAR_AWAY = 64.0
WIDE = 256
LIMIT = 56 * 1024 * 1024
F32 = jnp.float32
BF16 = jnp.bfloat16
VMEM = pl.BlockSpec(memory_space=pltpu.VMEM)
SMEM = pl.BlockSpec(memory_space=pltpu.SMEM)
PARAMS = pltpu.CompilerParams(vmem_limit_bytes=LIMIT)


def split3(x):
    first = x.astype(BF16).astype(F32)
    rest = x - first
    second = rest.astype(BF16).astype(F32)
    third = (rest - second).astype(BF16).astype(F32)
    return first, second, third


def split_table(table):
    return jnp.concatenate(split3(table), 0).astype(BF16)


def selectors(index, depth):
    count = index.shape[1]
    low = index & (WIDE - 1)
    high = index // WIDE
    hot = jnp.where(lax.broadcasted_iota(jnp.int32, (WIDE, count), 0) == low, 1.0, 0.0)
    mask = lax.broadcasted_iota(jnp.int32, (depth, count), 0) == high
    return hot.astype(BF16), mask


def pick(table, hot, mask):
    depth = mask.shape[0]
    size = table.shape[0] // 3
    parts = jnp.dot(table, hot, preferred_element_type=F32)
    whole = parts[:size] + parts[size : 2 * size] + parts[2 * size :]
    return [
        jnp.sum(jnp.where(mask, whole[row : row + depth], 0.0), 0, keepdims=True)
        for row in range(0, size, depth)
    ]


def spread(rows, hot, mask):
    firsts, seconds = [], []
    for row in rows:
        first = row.astype(BF16).astype(F32)
        firsts.append(jnp.where(mask, first, 0.0))
        seconds.append(jnp.where(mask, row - first, 0.0))
    stacked = jnp.concatenate(firsts + seconds, 0).astype(BF16)
    sums = lax.dot_general(stacked, hot, (((1,), (1,)), ((), ())), preferred_element_type=F32)
    half = sums.shape[0] // 2
    return sums[:half] + sums[half:]


def fold(ref, to_ref, first=0):
    rows, nodes = ref.shape
    depth = nodes // WIDE
    for row in range(rows):
        for high in range(depth):
            place = first + row * depth + high
            to_ref[place : place + 1, :] = ref[row : row + 1, high * WIDE : (high + 1) * WIDE]


def unfold(ref, to_ref):
    rows, nodes = to_ref.shape
    depth = nodes // WIDE
    for row in range(rows):
        for high in range(depth):
            place = row * depth + high
            to_ref[row : row + 1, high * WIDE : (high + 1) * WIDE] = ref[place : place + 1, :]


def lane_row(ref, start, count):
    tile = ref[pl.ds(pl.multiple_of(start, 8), count), :]
    return jnp.concatenate([tile[row : row + 1] for row in range(count)], 1)


def exchange(out_ref, got_ref, sent, received, kept):
    within = lax.axis_size("dev")
    count = lax.axis_size("grp") * within
    me = lax.axis_index("grp") * within + lax.axis_index("dev")

    def place(index):
        return {"grp": lax.div(index, within), "dev": lax.rem(index, within)}

    def copy(offset, landing):
        target = lax.rem(me + offset, count)
        return pltpu.make_async_remote_copy(
            src_ref=out_ref.at[target],
            dst_ref=got_ref.at[landing],
            send_sem=sent.at[offset],
            recv_sem=received.at[offset],
            device_id=place(target),
            device_id_type=pl.DeviceIdType.MESH,
        )

    barrier = pltpu.get_barrier_semaphore()

    def greet(offset, carry):
        target = lax.rem(me + offset, count)
        pl.semaphore_signal(
            barrier, 1, device_id=place(target), device_id_type=pl.DeviceIdType.MESH
        )
        return carry

    lax.fori_loop(1, count, greet, 0)
    own = pltpu.make_async_copy(out_ref.at[me], got_ref.at[me], kept)
    own.start()
    pl.semaphore_wait(barrier, count - 1)

    def start(offset, carry):
        copy(offset, me).start()
        return carry

    lax.fori_loop(1, count, start, 0)

    def finish():
        def wait(offset, carry):
            copy(offset, lax.rem(me + count - offset, count)).wait()
            return carry

        own.wait()
        lax.fori_loop(1, count, wait, 0)

    return finish


def segment_kernel(
    cap, pos_ref, disp_ref, seg_ref, mask_ref, send_ref, own_ref, out_ref, table_ref, moved_ref
):
    depth = table_ref.shape[0] // 3
    blocks, width = seg_ref.shape
    moved_ref[...] = pos_ref[...] + disp_ref[...]
    fold(moved_ref, table_ref)
    table = split_table(table_ref[...])

    many = math.gcd(blocks, 16)

    def gather(step, carry):
        start = step * many
        hot, mask = selectors(lane_row(seg_ref, start, many), depth)
        live = lane_row(mask_ref, start, many) > 0
        rows = [jnp.where(live, row, -FAR_AWAY) for row in pick(table, hot, mask)]
        square = rows[0] * rows[0] + rows[1] * rows[1] + rows[2] * rows[2]
        rows += [jnp.ones_like(square), -square]
        for block in range(many):
            lanes = slice(block * width, (block + 1) * width)
            for row in range(5):
                own_ref[start + block, row : row + 1, :] = rows[row][:, lanes]
            own_ref[start + block, 5:8, :] = jnp.zeros((3, width), F32)
        return carry

    lax.fori_loop(0, blocks // many, gather, 0)

    several = math.gcd(out_ref.shape[0], 8)

    def send(step, carry):
        for peer in [several * step + k for k in range(several)]:
            for slot in range(cap):
                block = own_ref[send_ref[peer * cap + slot], 0:3, :]
                out_ref[peer, 3 * slot : 3 * slot + 3, :] = jnp.where(
                    block < -0.5 * FAR_AWAY, FAR_AWAY, block
                )
            out_ref[peer, 3 * cap :, :] = jnp.zeros((out_ref.shape[1] - 3 * cap, width), F32)
        return carry

    lax.fori_loop(0, out_ref.shape[0] // several, send, 0)


def pull_kernel(
    chunk,
    disp_ref,
    mass_ref,
    nodes_ref,
    part_ref,
    scale_ref,
    stiff_ref,
    out_ref,
    pull_ref,
    ratio_ref,
    got_ref,
    table_ref,
    *semaphores,
):
    finish = exchange(out_ref, got_ref, *semaphores)
    depth = table_ref.shape[0] // 4
    elems = nodes_ref.shape[1]
    parts = stiff_ref.shape[0]
    fold(disp_ref, table_ref)
    fold(mass_ref, table_ref, 3 * depth)
    table = split_table(table_ref[...])

    def one_chunk(step, best):
        lanes = pl.ds(pl.multiple_of(step * chunk, chunk), chunk)
        local = lax.rem(part_ref[:, lanes], parts)
        stiff = jnp.zeros(local.shape, F32)
        for part in range(parts):
            stiff = jnp.where(local == part, stiff_ref[part], stiff)
        stiff = stiff * scale_ref[:, lanes]
        index = jnp.concatenate([nodes_ref[k : k + 1, lanes] for k in range(4)], 1)
        hot, mask = selectors(index, depth)
        rows = pick(table, hot, mask)
        corner = [[row[:, k * chunk : (k + 1) * chunk] for row in rows] for k in range(4)]
        mass = jnp.minimum(
            jnp.minimum(corner[0][3], corner[1][3]), jnp.minimum(corner[2][3], corner[3][3])
        )
        total = [[jnp.zeros_like(stiff) for axis in range(3)] for k in range(4)]
        for head, tail, weight in SPRINGS:
            for axis in range(3):
                pull = weight * stiff * (corner[tail][axis] - corner[head][axis])
                total[head][axis] = total[head][axis] + pull
                total[tail][axis] = total[tail][axis] - pull
        for axis in range(3):
            for k in range(4):
                pull_ref[4 * axis + k : 4 * axis + k + 1, lanes] = total[k][axis]
        return jnp.minimum(best, mass / stiff)

    best = lax.fori_loop(
        0, elems // chunk, one_chunk, jnp.full((1, chunk), jnp.inf, F32)
    )
    ratio_ref[...] = jnp.broadcast_to(jnp.min(best, 1, keepdims=True), ratio_ref.shape)
    finish()


def force_kernel(chunk, pull_ref, nodes_ref, out_ref, force_ref, got_ref, *semaphores):
    finish = exchange(out_ref, got_ref, *semaphores)
    depth = force_ref.shape[0] // 3
    force_ref[...] = jnp.zeros_like(force_ref)

    def one_chunk(step, carry):
        lanes = pl.ds(pl.multiple_of(step * chunk, chunk), chunk)
        index = jnp.concatenate([nodes_ref[k : k + 1, lanes] for k in range(4)], 1)
        hot, mask = selectors(index, depth)
        rows = [
            jnp.concatenate([pull_ref[4 * axis + k : 4 * axis + k + 1, lanes] for k in range(4)], 1)
            for axis in range(3)
        ]
        force_ref[...] += spread(rows, hot, mask)
        return carry

    lax.fori_loop(0, nodes_ref.shape[1] // chunk, one_chunk, 0)
    finish()


def pair_kernel(
    cap,
    group,
    own_ref,
    got_ref,
    ratio_ref,
    first_ref,
    second_ref,
    live_ref,
    seg_ref,
    back_ref,
    near_rows,
    near_turn,
    near_cols,
    far_rows,
    far_turn,
    far_cols,
    near_sum,
    far_sum,
    tile_ref,
):
    blocks, _, width = own_ref.shape
    peers = got_ref.shape[0]
    pairs = first_ref.shape[0]
    scale = 2.0

    row_id = lax.broadcasted_iota(jnp.int32, (8, width), 0)
    pad = jnp.zeros((16, width), BF16)
    gap = jnp.zeros((64, width), BF16)

    def operands(tile):
        one, two, three = split3(tile)
        mixed = jnp.where(row_id < 3, two, pltpu.roll(three, 3, 0))
        mixed = jnp.where(row_id < 6, mixed, 0.0)
        columns = jnp.concatenate([one, mixed], 0)
        return one, two, three, jnp.concatenate([columns, columns], 1).astype(BF16)

    def prepare_near(step, carry):
        for member in range(8):
            block = 8 * step + member
            one, two, three, columns = operands(own_ref[block])
            rows = jnp.concatenate([one, one, two, two, one, three], 0).astype(BF16)
            rows = jnp.concatenate([rows, pad], 0)
            near_rows[block] = rows
            near_turn[block] = jnp.concatenate([rows, gap], 0).T
            near_cols[block] = columns
            near_sum[block] = jnp.zeros((16, width), F32)
        return carry

    lax.fori_loop(0, blocks // 8, prepare_near, 0)

    tile_ref[...] = jnp.zeros_like(tile_ref)

    several = math.gcd(peers, 4)

    def prepare_far(step, carry):
        places = [(several * step + k, slot) for k in range(several) for slot in range(cap)]
        for member, (peer, slot) in enumerate(places):
            tile_ref[member, 0:3, :] = got_ref[peer, 3 * slot : 3 * slot + 3, :]
        for member, (peer, slot) in enumerate(places):
            tile = tile_ref[member]
            square = -jnp.sum(tile * tile, 0, keepdims=True)
            one, two, three, columns = operands(
                jnp.where(row_id == 3, square, jnp.where(row_id == 4, 1.0, scale * tile))
            )
            place = peer * cap + slot
            rows = jnp.concatenate([one, two, one, two, three, one], 0).astype(BF16)
            rows = jnp.concatenate([rows, pad], 0)
            far_rows[place] = rows
            far_turn[place] = jnp.concatenate([gap, rows], 0).T
            far_cols[place] = columns
            far_sum[place] = jnp.zeros((16, width), F32)
        return carry

    lax.fori_loop(0, peers // several, prepare_far, 0)

    def one_group(step, carry):
        results = []
        for member in range(group):
            place = step * group + member
            near, far = first_ref[place], second_ref[place]
            live = live_ref[place].astype(F32)
            right = jnp.concatenate(
                [
                    jnp.concatenate([far_rows[far], gap], 1),
                    jnp.concatenate([gap, near_rows[near]], 1),
                ],
                0,
            )
            both = jnp.dot(
                near_turn[near] + far_turn[far], right, preferred_element_type=F32
            )
            weight = jnp.exp(both)
            first = weight.astype(BF16)
            second = (weight - first.astype(F32)).astype(BF16)
            sums = jnp.dot(
                jnp.concatenate([near_cols[near], far_cols[far]], 0),
                jnp.concatenate([first, second], 0),
                preferred_element_type=F32,
            )
            results.append((near, far, live * sums[16:, width:], live * sums[:16, :width]))
        for near, far, pushed, recoil in results:
            near_sum[near] += pushed
            far_sum[far] += recoil
        return carry

    lax.fori_loop(0, pairs // group, one_group, 0)

    def joined(sums):
        low = sums[8:16]
        return sums[:8] + jnp.where(row_id < 3, low + pltpu.roll(low, 5, 0), 0.0)

    def finish_near(step, carry):
        for member in range(8):
            block = 8 * step + member
            sums = joined(near_sum[block])
            seg_ref[block] = own_ref[block] * sums[4:5] - (1.0 / scale) * sums
        return carry

    lax.fori_loop(0, blocks // 8, finish_near, 0)

    def finish_far(step, carry):
        for peer in [several * step + k for k in range(several)]:
            for slot in range(cap):
                rows = slice(3 * slot, 3 * slot + 3)
                sums = joined(far_sum[peer * cap + slot])
                back_ref[peer, rows, :] = got_ref[peer, rows, :] * sums[3:4] - sums[0:3]
            back_ref[peer, 3 * cap :, :] = jnp.broadcast_to(
                ratio_ref[0:1], (back_ref.shape[1] - 3 * cap, width)
            )
        return carry

    lax.fori_loop(0, peers // several, finish_far, 0)


def total_kernel(
    cap,
    chunk,
    back_ref,
    send_ref,
    own_ref,
    seg_ref,
    force_ref,
    shared_ref,
    total_ref,
    lower_ref,
    upper_ref,
    step_ref,
    sums,
):
    depth = force_ref.shape[0] // 3
    blocks, width = seg_ref.shape
    sums[...] = own_ref[...]

    peers = back_ref.shape[0]
    several = math.gcd(peers, 8)

    def give_back(step, best):
        for peer in [several * step + k for k in range(several)]:
            for slot in range(cap):
                block = send_ref[peer * cap + slot]
                sums[block, 0:3, :] += back_ref[peer, 3 * slot : 3 * slot + 3, :]
            best = jnp.minimum(best, back_ref[peer, 3 * cap : 3 * cap + 1, :])
        return best

    best = lax.fori_loop(
        0, peers // several, give_back, jnp.full((1, width), jnp.inf, F32)
    )
    step_ref[...] = jnp.broadcast_to(COURANT * jnp.sqrt(best), step_ref.shape)
    total_ref[...] = force_ref[...]

    many = math.gcd(blocks, 16)

    def scatter(step, carry):
        start = step * many
        hot, mask = selectors(lane_row(seg_ref, start, many), depth)
        rows = [
            jnp.concatenate([sums[start + block, row : row + 1, :] for block in range(many)], 1)
            for row in range(3)
        ]
        total_ref[...] += spread(rows, hot, mask)
        return carry

    lax.fori_loop(0, blocks // many, scatter, 0)

    table = split_table(total_ref[...])

    def gather(step, carry):
        lanes = pl.ds(pl.multiple_of(step * chunk, chunk), chunk)
        index = jnp.concatenate([shared_ref[side : side + 1, lanes] for side in range(2)], 1)
        rows = pick(table, *selectors(index, depth))
        for row in range(3):
            upper_ref[row : row + 1, lanes] = rows[row][:, :chunk]
            lower_ref[row : row + 1, lanes] = rows[row][:, chunk:]
        return carry

    lax.fori_loop(0, shared_ref.shape[1] // chunk, gather, 0)


def update_kernel(
    chunk,
    total_ref,
    lower_ref,
    upper_ref,
    shared_ref,
    mass_ref,
    vel_ref,
    disp_ref,
    step_ref,
    new_disp_ref,
    new_vel_ref,
    sums,
    got_lower,
    got_upper,
    sent,
    received,
):
    me = lax.axis_index("dev")
    last = lax.axis_size("dev") - 1
    prev = {"dev": jnp.maximum(me - 1, 0)}
    following = {"dev": jnp.minimum(me + 1, last)}
    upward = pltpu.make_async_remote_copy(
        src_ref=lower_ref,
        dst_ref=got_lower,
        send_sem=sent.at[0],
        recv_sem=received.at[0],
        device_id=following,
        device_id_type=pl.DeviceIdType.MESH,
    )
    downward = pltpu.make_async_remote_copy(
        src_ref=upper_ref,
        dst_ref=got_upper,
        send_sem=sent.at[1],
        recv_sem=received.at[1],
        device_id=prev,
        device_id_type=pl.DeviceIdType.MESH,
    )
    barrier = pltpu.get_barrier_semaphore()

    @pl.when(me > 0)
    def _():
        pl.semaphore_signal(barrier, 1, device_id=prev, device_id_type=pl.DeviceIdType.MESH)

    @pl.when(me < last)
    def _():
        pl.semaphore_signal(barrier, 1, device_id=following, device_id_type=pl.DeviceIdType.MESH)

    pl.semaphore_wait(barrier, jnp.minimum(me, 1) + jnp.minimum(last - me, 1))

    @pl.when(me < last)
    def _():
        upward.start()

    @pl.when(me > 0)
    def _():
        downward.start()

    sums[...] = total_ref[...]
    depth = sums.shape[0] // 3

    @pl.when(me == 0)
    def _():
        got_lower[...] = jnp.zeros_like(got_lower)

    @pl.when(me == last)
    def _():
        got_upper[...] = jnp.zeros_like(got_upper)

    @pl.when(me > 0)
    def _():
        upward.wait_recv()

    @pl.when(me < last)
    def _():
        downward.wait_recv()

    def scatter(step, carry):
        lanes = pl.ds(pl.multiple_of(step * chunk, chunk), chunk)
        index = jnp.concatenate([shared_ref[side : side + 1, lanes] for side in range(2)], 1)
        rows = [
            jnp.concatenate([got_lower[row : row + 1, lanes], got_upper[row : row + 1, lanes]], 1)
            for row in range(3)
        ]
        sums[...] += spread(rows, *selectors(index, depth))
        return carry

    lax.fori_loop(0, shared_ref.shape[1] // chunk, scatter, 0)
    unfold(sums, new_vel_ref)
    time_step = step_ref[0:1, 0:1]
    velocity = vel_ref[...] + time_step * (new_vel_ref[...] / mass_ref[...])
    new_vel_ref[...] = velocity
    new_disp_ref[...] = disp_ref[...] + time_step * velocity

    @pl.when(me < last)
    def _():
        upward.wait_send()

    @pl.when(me > 0)
    def _():
        downward.wait_send()


def shape(*dims):
    return jax.ShapeDtypeStruct(dims, F32)


def shards(
    ref_pos,
    displacement,
    velocity,
    node_mass,
    elem_nodes,
    elem_part,
    elem_scale,
    part_stiff,
    shared,
    seg_node,
    seg_mask,
    send_blk,
    pair_a,
    pair_slot,
    pair_mask,
):
    peers, cap = send_blk.shape[1:]
    nodes = node_mass.shape[0]
    blocks, width = seg_node.shape
    elems = elem_nodes.shape[1]
    pairs = pair_a.shape[0]
    share = shared.shape[1]
    depth = nodes // WIDE
    slab = -(-(3 * cap + 1) // 8) * 8
    mass = node_mass.reshape(1, -1)
    send = send_blk.reshape(-1)

    own, outgoing = pl.pallas_call(
        functools.partial(segment_kernel, cap),
        out_shape=(shape(blocks, 8, width), shape(peers, slab, width)),
        in_specs=[VMEM, VMEM, VMEM, VMEM, SMEM],
        out_specs=(VMEM, VMEM),
        scratch_shapes=[pltpu.VMEM((3 * depth, WIDE), F32), pltpu.VMEM((3, nodes), F32)],
        compiler_params=PARAMS,
        name="segments",
    )(ref_pos, displacement, seg_node, seg_mask, send)

    chunk = math.gcd(elems, 1024)
    work = 2 * 4 * elems * WIDE * depth
    semaphores = [
        pltpu.SemaphoreType.DMA((peers,)),
        pltpu.SemaphoreType.DMA((peers,)),
        pltpu.SemaphoreType.DMA,
    ]
    pull, ratio, arrived = pl.pallas_call(
        functools.partial(pull_kernel, chunk),
        out_shape=(shape(12, elems), shape(8, width), shape(peers, slab, width)),
        in_specs=[VMEM, VMEM, VMEM, VMEM, VMEM, SMEM, VMEM],
        out_specs=(VMEM, VMEM, VMEM),
        scratch_shapes=[pltpu.VMEM((4 * depth, WIDE), F32)] + semaphores,
        compiler_params=pltpu.CompilerParams(
            vmem_limit_bytes=LIMIT, collective_id=1, has_side_effects=True
        ),
        cost_estimate=pl.CostEstimate(flops=12 * work, bytes_accessed=2**20, transcendentals=0),
        name="pulls",
    )(displacement, mass, elem_nodes, elem_part.reshape(1, -1), elem_scale.reshape(1, -1), part_stiff, outgoing)

    group = math.gcd(pairs, 64)
    seg_force, going_back = pl.pallas_call(
        functools.partial(pair_kernel, cap, group),
        out_shape=(shape(blocks, 8, width), shape(peers, slab, width)),
        in_specs=[VMEM, VMEM, VMEM, SMEM, SMEM, SMEM],
        out_specs=(VMEM, VMEM),
        scratch_shapes=[
            pltpu.VMEM((blocks, 64, width), BF16),
            pltpu.VMEM((blocks, width, width), BF16),
            pltpu.VMEM((blocks, 16, 2 * width), BF16),
            pltpu.VMEM((peers * cap, 64, width), BF16),
            pltpu.VMEM((peers * cap, width, width), BF16),
            pltpu.VMEM((peers * cap, 16, 2 * width), BF16),
            pltpu.VMEM((blocks, 16, width), F32),
            pltpu.VMEM((peers * cap, 16, width), F32),
            pltpu.VMEM((4 * cap, 8, width), F32),
        ],
        compiler_params=PARAMS,
        name="pairs",
    )(own, arrived, ratio, pair_a, pair_slot, pair_mask)

    force, returned = pl.pallas_call(
        functools.partial(force_kernel, chunk),
        out_shape=(shape(3 * depth, WIDE), shape(peers, slab, width)),
        in_specs=[VMEM, VMEM, VMEM],
        out_specs=(VMEM, VMEM),
        scratch_shapes=semaphores,
        compiler_params=pltpu.CompilerParams(
            vmem_limit_bytes=LIMIT, collective_id=2, has_side_effects=True
        ),
        cost_estimate=pl.CostEstimate(flops=12 * work, bytes_accessed=2**20, transcendentals=0),
        name="forces",
    )(pull, elem_nodes, going_back)

    piece = math.gcd(share, 2048)
    total, lower, upper, time_step = pl.pallas_call(
        functools.partial(total_kernel, cap, piece),
        out_shape=(shape(3 * depth, WIDE), shape(3, share), shape(3, share), shape(8, width)),
        in_specs=[VMEM, SMEM, VMEM, VMEM, VMEM, VMEM],
        out_specs=(VMEM, VMEM, VMEM, VMEM),
        scratch_shapes=[pltpu.VMEM((blocks, 8, width), F32)],
        compiler_params=PARAMS,
        name="totals",
    )(returned, send, seg_force, seg_node, force, shared)

    return pl.pallas_call(
        functools.partial(update_kernel, piece),
        out_shape=(shape(3, nodes), shape(3, nodes)),
        in_specs=[VMEM] * 8,
        out_specs=(VMEM, VMEM),
        scratch_shapes=[
            pltpu.VMEM((3 * depth, WIDE), F32),
            pltpu.VMEM((3, share), F32),
            pltpu.VMEM((3, share), F32),
            pltpu.SemaphoreType.DMA((2,)),
            pltpu.SemaphoreType.DMA((2,)),
        ],
        compiler_params=pltpu.CompilerParams(
            vmem_limit_bytes=LIMIT, collective_id=0, has_side_effects=True
        ),
        name="update",
    )(total, lower, upper, shared, mass, velocity, displacement, time_step)


def solution(mesh):
    return jax.shard_map(
        shards,
        mesh=mesh,
        in_specs=(
            P(None, ("grp", "dev")),
            P(None, ("grp", "dev")),
            P(None, ("grp", "dev")),
            P(("grp", "dev")),
            P(None, ("grp", "dev")),
            P(("grp", "dev")),
            P(("grp", "dev")),
            P(("grp", "dev")),
            P(None, ("grp", "dev")),
            P(("grp", "dev"), None),
            P(("grp", "dev"), None),
            P(("grp", "dev"), None, None),
            P(("grp", "dev")),
            P(("grp", "dev")),
            P(("grp", "dev")),
        ),
        out_specs=(P(None, ("grp", "dev")), P(None, ("grp", "dev"))),
        check_vma=False,
    )
```
